256 devices in a mesh: space: 64 (over z, x, core), inst: 4 (over y).
Axes of the slice: x: 4, y: 4, z: 8, core: 2. Of those that a mesh axis runs over, the one named last changes fastest.
Arguments:
- start: float32 [16, 7, 131072], P('inst', None, 'space'), may hold values from -14 to 14
- shifted_diag: float32 [131072], P('space'), may hold values from -1 to 1
- face_coef: float32 [6, 131072], P(None, 'space'), may hold values from 0.03 to 0.15
- mixing: float32 [7, 7], replicated, may hold values from -2 to 2
- neighbours: int32 [6, 131072], P(None, 'space'), may hold values from 0 to 2559, as said below
- basis: float32 [20, 16, 7, 131072], P(None, 'inst', None, 'space'), may hold values from -13 to 13
Outputs:
- block: float32 [4, 16, 7, 131072], P(None, 'inst', None, 'space')
- proj: float32 [20, 4], replicated
- factor: float32 [4, 4], replicated
The draws below stay inside these ranges and needn't reach their ends.
Inputs may be any that keep to these rules, and one draw needn't show every extreme that they name: `neighbours`: faces 0 and 1 of a cell name the cell one layer below and above it; faces 2 to 5 name cells of the same layer.
All inputs are finite; a program needn't handle non-finite values.
Results may differ from the reference program's by a relative error of at most 0.00026.
Values sent between devices are 32-bit elements; how exact they have to be, the bound alone decides.
A program may use at most 64 MiB of HBM per device.

```python
import math
import jax
import jax.numpy as jnp
from jax import lax

NT = 16
VARS = 7
NB = 20
S = 4
FACES = 6
FACE = 256
CELL_DEV = 2048
CELLS = 131072


aligned_weight = 0.916515


jitter_weight = 0.4


def mixed_law(key, extent):
    normal_key = jax.random.fold_in(key, 31)
    normal_part = jax.random.truncated_normal(normal_key, -4.0, 4.0, extent, jnp.float32)
    return normal_part


def cell_position(key):
    return jax.random.uniform(jax.random.fold_in(key, 901), (CELLS,), jnp.float32, -1.0, 1.0)


def group_fields(key):
    return mixed_law(jax.random.fold_in(key, 902), (NB // (S + 1), NT, VARS, CELLS))


def legendre_table(position):
    levels = [jnp.ones_like(position), position]
    for degree in range(1, S):
        levels.append(((2 * degree + 1) * position * levels[degree] - degree * levels[degree - 1]) / (degree + 1))
    scaled = [levels[degree] * math.sqrt(2 * degree + 1) for degree in range(S + 1)]
    return jnp.stack(scaled)


def draw_shifted_diag(key, part):
    position = cell_position(key)
    return position


def draw_basis(key, part):
    position = cell_position(key)
    fields = group_fields(key)
    key = jax.random.fold_in(key, 13)
    legendre = legendre_table(position)
    aligned = legendre[None, :, None, None, :] * fields[:, None, :, :, :]
    jitter = mixed_law(key, (NB, NT, VARS, CELLS))
    return aligned_weight * aligned.reshape(NB, NT, VARS, CELLS) + jitter_weight * jitter


def draw_start(key, part):
    fields = group_fields(key)
    key = jax.random.fold_in(key, 17)
    weight_key = jax.random.fold_in(key, 1)
    sign_key = jax.random.fold_in(key, 2)
    jitter_key = jax.random.fold_in(key, 3)
    groups = NB // (S + 1)
    signs = jnp.where(jax.random.bernoulli(sign_key, 0.5, (groups,)), 1.0, -1.0).astype(jnp.float32)
    weights = jax.random.uniform(weight_key, (groups,), jnp.float32, 0.3, 0.7) * signs
    combined = jnp.sum(weights[:, None, None, None] * fields, axis=0)
    return combined + 0.5 * mixed_law(jitter_key, (NT, VARS, CELLS))


def draw_neighbours(key, part):
    key = jax.random.fold_in(key, 7)
    local = jnp.arange(CELLS, dtype=jnp.int32) % CELL_DEV
    layer = local // FACE
    below = local
    above = local + 2 * FACE
    within = FACE + layer[None, :] * FACE + jax.random.randint(key, (4, CELLS), 0, FACE, dtype=jnp.int32)
    return jnp.concatenate([below[None, :], above[None, :], within], axis=0).astype(jnp.int32)


def block_scale(own_key, dims, split, least, high):
    loudness, own = 1.0, jax.random.fold_in(own_key, 6)
    for dim, parts in split:
        steps = jnp.exp(jax.random.uniform(jax.random.fold_in(own, dim), (parts,), jnp.float32, least / len(split), high / len(split)))
        loudness = loudness * jnp.repeat(steps, dims[dim] // parts).reshape([-1 if axis == dim else 1 for axis in range(len(dims))])
    return loudness


def normal_values(stream_key, dims, deviation, most, kind=jnp.bfloat16):
    return jnp.clip(deviation * jax.random.normal(stream_key, dims, jnp.float32), -most, most).astype(kind)


def setup_inputs(seed: int = 0) -> dict:
    key_list = jax.random.split(jax.random.key(seed), 7)
    start = draw_start(jax.random.fold_in(key_list[6], 71), 0)
    shifted_diag = draw_shifted_diag(jax.random.fold_in(key_list[6], 71), 0)
    face_coef = jnp.clip(jnp.exp(math.log(0.15) - 1.609438 * jax.random.uniform(key_list[2], (FACES, CELLS), jnp.float32) ** block_scale(key_list[2], (FACES, CELLS), ((1, 64),), -0.2, 0.2)), 0.03, 0.15)
    mixing = normal_values(key_list[3], (VARS, VARS), VARS ** -0.5, 2.0, jnp.float32)
    neighbours = draw_neighbours(jax.random.fold_in(key_list[6], 71), 0)
    basis = draw_basis(jax.random.fold_in(key_list[6], 71), 0)
    return {"start": start, "shifted_diag": shifted_diag, "face_coef": face_coef, "mixing": mixing, "neighbours": neighbours, "basis": basis}


def spectral_rows(rows, cols):
    idiff = rows[:, None] - cols[None, :]
    angle = idiff.astype(jnp.float32) * jnp.float32(math.pi / NT)
    parity = jnp.where(idiff % 2 == 0, jnp.float32(1.0), jnp.float32(-1.0))
    safe = jnp.where(idiff == 0, jnp.float32(1.0), jnp.sin(angle))
    return jnp.where(idiff == 0, jnp.float32(0.0), 0.5 * parity * jnp.cos(angle) / safe)

def apply_operator(field, shifted_diag, face_coef, mixing, neighbours):
    padded = jnp.pad(field, ((0, 0), (0, 0), (FACE, FACE)))
    owner = jnp.arange(CELLS, dtype=jnp.int32) // CELL_DEV * CELL_DEV
    global_nb = neighbours + owner[None, :]
    flux = jnp.zeros_like(field)
    for face in range(FACES):
        flux = flux + face_coef[face] * (field - padded[:, :, global_nb[face]])
    mixed = jnp.einsum('ij,njc->nic', mixing, flux, precision=lax.Precision.HIGHEST)
    steps_idx = jnp.arange(NT, dtype=jnp.int32)
    dmat = spectral_rows(steps_idx, steps_idx)
    timed = 0.1 * jnp.einsum('nk,kjc->njc', dmat, field, precision=lax.Precision.HIGHEST)
    return shifted_diag * field + timed + mixed

def reference(start, shifted_diag, face_coef, mixing, neighbours, basis):
    current = start
    vectors = []
    for step in range(S):
        current = apply_operator(current, shifted_diag, face_coef, mixing, neighbours)
        vectors.append(current)
    krylov = jnp.stack(vectors)
    total_count = jnp.float32(NT * VARS * CELLS)
    proj = jnp.einsum('bnjc,snjc->bs', basis, krylov, precision=lax.Precision.HIGHEST) / total_count
    projected = krylov - jnp.einsum('bs,bnjc->snjc', proj, basis, precision=lax.Precision.HIGHEST)
    gram = jnp.einsum('snjc,tnjc->st', projected, projected, precision=lax.Precision.HIGHEST) / total_count
    lower = jnp.linalg.cholesky(gram)
    inverse = jax.scipy.linalg.solve_triangular(lower, jnp.eye(S, dtype=jnp.float32), lower=True)
    block = jnp.einsum('st,tnjc->snjc', inverse, projected, precision=lax.Precision.HIGHEST)
    return (block, proj, lower.T)
```

```python
import math

import jax
import jax.numpy as jnp
import numpy as np
from jax import lax
from jax.experimental import pallas as pl
from jax.experimental.pallas import tpu as pltpu
from jax.sharding import PartitionSpec as P

NT = 16
VARS = 7
NB = 20
S = 4
FACES = 6
FACE = 256
LAYERS = 8
NZ = NB + S
WIDE = 16
MESH = pl.DeviceIdType.MESH
F32 = jnp.float32
BF16 = jnp.bfloat16
TOTAL = float(NT * VARS * 131072)

GATHER = lax.GatherDimensionNumbers(
    offset_dims=(),
    collapsed_slice_dims=(1,),
    start_index_map=(1,),
    operand_batching_dims=(0,),
    start_indices_batching_dims=(0,),
)


def time_tables():
    n = np.arange(NT)
    diff = n[:, None] - n[None, :]
    angle = np.where(diff == 0, 1.0, np.pi * diff / NT)
    dmat = np.where(diff == 0, 0.0, 0.5 * (-1.0) ** diff * np.cos(angle) / np.sin(angle))
    tables = np.zeros((4, 8 * S, 8 * S))
    for d in range(4):
        for k in range(1, S + 1):
            for j in range(k):
                power = np.linalg.matrix_power(0.1 * dmat, k - j)
                part = math.comb(k, j) * power[:4, 4 * d : 4 * d + 4]
                for half in range(2):
                    r, c = (k - 1) * 8 + half * 4, j * 8 + half * 4
                    tables[d, r : r + 4, c : c + 4] = part
    high = tables.astype(jnp.bfloat16).astype(np.float64)
    low = (tables - high).astype(jnp.bfloat16).astype(np.float64)
    return np.concatenate([high, high, low], axis=2).astype(np.float32)


def take(x, index):
    return lax.gather(
        x, index[:, :, None], GATHER, slice_sizes=(1, 1), mode=lax.GatherScatterMode.PROMISE_IN_BOUNDS
    )


def kernel(
    start, coef, near, diag, basis, mixing, times,
    block, proj, factor,
    u, u4, w, bas, coef_own, near_own, diag_own, coef_side, near_side, diag_side,
    geo, seat, mix, acc, cf, slots,
    load_sem, ys, yr, xs, xr, gs, gr, out_sem, as_, ar,
):
    p, q = lax.axis_index("space"), lax.axis_index("inst")
    z, x, c = p // 8, (p // 2) % 4, p % 2
    has_low, has_high = p > 0, p < 63
    y_up, y_down = (q + 1) % 4, (q + 3) % 4

    def group_peer(phase, m):
        if phase == 0:
            return {"space": (z * 4 + m // 4) * 2 + c, "inst": m % 4}
        return {"space": ((m // 2) * 4 + x) * 2 + m % 2, "inst": q}

    mine = (x * 4 + q, z * 2 + c)

    loads = [
        pltpu.make_async_copy(coef, coef_own, load_sem.at[0]),
        pltpu.make_async_copy(near, near_own, load_sem.at[1]),
        pltpu.make_async_copy(diag, diag_own, load_sem.at[2]),
        pltpu.make_async_copy(start, u.at[0, 0, :, pl.ds(4, LAYERS)], load_sem.at[3]),
        pltpu.make_async_copy(basis, bas, load_sem.at[4]),
    ]
    for copy in loads:
        copy.start()

    barrier = pltpu.get_barrier_semaphore()

    def greet(phase):
        def body(i, carry):
            pl.semaphore_signal(
                barrier, inc=1, device_id=group_peer(phase, (mine[phase] + i) % 16), device_id_type=MESH
            )
            return carry

        lax.fori_loop(1, 16, body, 0)

    greet(0)
    greet(1)

    @pl.when(has_low)
    def _():
        pl.semaphore_signal(barrier, inc=1, device_id={"space": p - 1, "inst": q}, device_id_type=MESH)

    @pl.when(has_high)
    def _():
        pl.semaphore_signal(barrier, inc=1, device_id={"space": p + 1, "inst": q}, device_id_type=MESH)

    pl.semaphore_wait(barrier, 30 + jnp.where(has_low, 1, 0) + jnp.where(has_high, 1, 0))

    def y_copy(d, h):
        dst = u.at[0, d, :, pl.ds(4 + 4 * h, 4)]
        if d == 2:
            src = u.at[0, 3 if h == 0 else 1, :, pl.ds(4 + 4 * h, 4)]
            to = y_up if h == 0 else y_down
        else:
            src = start.at[:, pl.ds(4 * h, 4)]
            to = y_up if d == 3 else y_down
        return pltpu.make_async_remote_copy(
            src, dst, ys.at[d, h], yr.at[d, h], device_id={"space": p, "inst": to}, device_id_type=MESH
        )

    def x_copy(d, side):
        count = 4 if d == 0 else 3
        if side == 0:
            dst = u.at[0, d, :, pl.ds(4 - count, count)]
            src = start.at[:, pl.ds(8 - count, count)] if d == 0 else u.at[0, d, :, pl.ds(12 - count, count)]
            to = p + 1
        else:
            dst = u.at[0, d, :, pl.ds(12, count)]
            src = start.at[:, pl.ds(0, count)] if d == 0 else u.at[0, d, :, pl.ds(4, count)]
            to = p - 1
        return pltpu.make_async_remote_copy(
            src, dst, xs.at[d, side], xr.at[d, side], device_id={"space": to, "inst": q}, device_id_type=MESH
        )

    def side_copies(side):
        to = p + 1 if side == 0 else p - 1
        cut = pl.ds(5 * FACE, 3 * FACE) if side == 0 else pl.ds(0, 3 * FACE)
        pairs = (
            (coef.at[:, cut], coef_side.at[side]),
            (near.at[:, cut], near_side.at[side]),
            (diag, diag_side.at[side]),
        )
        return [
            pltpu.make_async_remote_copy(
                src, dst, gs.at[side, i], gr.at[side, i], device_id={"space": to, "inst": q}, device_id_type=MESH
            )
            for i, (src, dst) in enumerate(pairs)
        ]

    sends = (has_high, has_low)
    hears = (has_low, has_high)

    def x_start(d, side):
        @pl.when(sends[side])
        def _():
            x_copy(d, side).start()

    y_copy(3, 0).start()
    y_copy(1, 1).start()
    for side in range(2):

        @pl.when(sends[side])
        def _():
            for copy in side_copies(side):
                copy.start()

        x_start(0, side)
    y_copy(3, 1).start()
    y_copy(1, 0).start()

    for side in range(2):

        @pl.when(jnp.logical_not(hears[side]))
        def _():
            coef_side[side] = jnp.zeros((FACES, 3 * FACE), F32)
            near_side[side] = jnp.zeros((FACES, 3 * FACE), jnp.int32)
            diag_side[side] = jnp.zeros((16, 128), F32)
            for d in range(4):
                first = 0 if side == 0 else 12
                u[0, d, :, pl.ds(first, 4)] = jnp.zeros((VARS, 4, 8, 128), F32)

    sub = lax.broadcasted_iota(jnp.int32, (8, 128), 0)
    lane = lax.broadcasted_iota(jnp.int32, (8, 128), 1)
    upper = sub >= 4

    for i in range(VARS):
        for j in range(VARS):
            mix[i * VARS + j] = jnp.full((8, 128), mixing[i, j], F32)

    for copy in loads[:3]:
        copy.wait()

    def spread(values, at):
        first = jnp.broadcast_to(values[:, at : at + 128], (8, 128))
        second = jnp.broadcast_to(values[:, at + 128 : at + 256], (8, 128))
        return jnp.where(upper, second, first)

    def place(layer, coefs, nears, at, diags):
        total = None
        for f in range(FACES):
            value = spread(coefs[f : f + 1], at)
            geo[1 + f, layer] = value
            total = value if total is None else total + value
        geo[0, layer] = total
        geo[7, layer] = jnp.where(
            upper, jnp.broadcast_to(diags[1:2], (8, 128)), jnp.broadcast_to(diags[0:1], (8, 128))
        )
        for f in range(2, FACES):
            seat[f - 2, layer] = spread(nears[f : f + 1], at) & (FACE - 1)

    coefs, nears, diags = coef_own[...], near_own[...], diag_own[...]
    for layer in range(LAYERS):
        place(4 + layer, coefs, nears, layer * FACE, diags[2 * layer : 2 * layer + 2])
    for side in range(2):

        @pl.when(hears[side])
        def _():
            for copy in side_copies(side):
                copy.wait_recv()

        coefs, nears, diags = coef_side[side], near_side[side], diag_side[side]
        for layer in range(3):
            first = 10 + 2 * layer if side == 0 else 2 * layer
            place((1 if side == 0 else 12) + layer, coefs, nears, layer * FACE, diags[first : first + 2])

    def step(src, dst, low, high):
        def pair(i, carry):
            a = low + 2 * i
            values, fluxes = [], []
            for e in range(2):
                g = [geo[f, a + e] for f in range(7)]
                lanes, same = [], []
                for f in range(4):
                    seats = seat[f, a + e]
                    lanes.append(seats & 127)
                    same.append((seats >= 128) == upper)
                for v in range(VARS):
                    center = src[v, a + e]
                    other = pltpu.roll(center, 4, 0)
                    flux = g[0] * center - g[1] * src[v, a + e - 1] - g[2] * src[v, a + e + 1]
                    for f in range(4):
                        value = jnp.where(same[f], take(center, lanes[f]), take(other, lanes[f]))
                        flux = flux - g[3 + f] * value
                    fluxes.append(flux)
            d0, d1 = geo[7, a], geo[7, a + 1]
            for i in range(VARS):
                r0, r1 = d0 * src[i, a], d1 * src[i, a + 1]
                for j in range(VARS):
                    m = mix[i * VARS + j]
                    r0 = r0 + m * fluxes[j]
                    r1 = r1 + m * fluxes[VARS + j]
                dst[i, a], dst[i, a + 1] = r0, r1
            return carry

        lax.fori_loop(0, (high - low) // 2, pair, 0)

    def chain(d):
        low = 1 if d == 0 else 2
        for j in range(3):
            step(u.at[j, d], u.at[j + 1, d], low + j, 16 - low - j)
        if d == 0:
            step(u.at[3, 0], u4, 4, 12)

    def combine(d):
        table = times[d].astype(BF16)

        def body(i, carry):
            v, l = i // 4, 2 * (i % 4)
            columns = []
            for e in range(2):
                parts = jnp.concatenate([u[j, d, v, 4 + l + e] for j in range(S)], axis=0)
                high = parts.astype(BF16)
                low = (parts - high.astype(F32)).astype(BF16)
                columns.append(jnp.concatenate([high, low, high], axis=0))
            out = jnp.dot(table, jnp.concatenate(columns, axis=1), preferred_element_type=F32)
            for e in range(2):
                for k in range(S):
                    term = out[8 * k : 8 * k + 8, 128 * e : 128 * e + 128]
                    if d == 0:
                        last = u4[v, 4 + l + e] if k == S - 1 else u[k + 1, 0, v, 4 + l + e]
                        w[k, v, l + e] = last + term
                    else:
                        w[k, v, l + e] += term
            return carry

        lax.fori_loop(0, VARS * 4, body, 0)

    def products(left, right, pairs, places):
        def body(i, sums):
            v, l = i // LAYERS, i % LAYERS
            a = {k: r[n, v, l] for k, (r, n) in left.items()}
            b = {k: r[n, v, l] for k, (r, n) in right.items()}
            return tuple(s + a[m] * b[n] for s, (m, n) in zip(sums, pairs))

        zero = jnp.zeros((8, 128), F32)
        sums = lax.fori_loop(0, VARS * LAYERS, body, (zero,) * len(pairs))
        for total, spots in zip(sums, places):
            for row, column in spots:
                acc[pl.ds((column * NZ + row) * 8, 8)] = total

    def basis_block(i, j):
        pairs = [(a, b) for a in range(5 * i, 5 * i + 5) for b in range(5 * j, 5 * j + 5) if a <= b]
        products(
            {a: (bas, a) for a in range(5 * i, 5 * i + 5)},
            {b: (bas, b) for b in range(5 * j, 5 * j + 5)},
            pairs,
            [((a, b), (b, a)) if a != b else ((a, b),) for a, b in pairs],
        )

    def gather_sums(columns):
        wide = lax.broadcasted_iota(jnp.int32, (NZ, 128), 1)
        result = jnp.zeros((NZ, 128), F32)
        for column in columns:
            rows = acc[pl.ds(column * NZ * 8, NZ, stride=8)]
            for s in range(1, 8):
                rows = rows + acc[pl.ds(column * NZ * 8 + s, NZ, stride=8)]
            result = jnp.where(wide == column, jnp.sum(rows, axis=1, keepdims=True), result)
        return result

    def x_wait(d):
        for side in range(2):

            @pl.when(hears[side])
            def _():
                x_copy(d, side).wait_recv()

    loads[3].wait()
    x_wait(0)
    chain(0)
    combine(0)

    y_copy(3, 0).wait_recv()
    y_copy(2, 0).start()
    y_copy(1, 1).wait_recv()
    y_copy(2, 1).start()
    x_start(3, 1)
    x_start(1, 0)

    loads[4].wait()
    todo = [(i, j) for i in range(4) for j in range(i, 4)]
    for i, j in todo[:4]:
        basis_block(i, j)

    y_copy(3, 1).wait_recv()
    x_start(3, 0)
    y_copy(1, 0).wait_recv()
    x_start(1, 1)

    for i, j in todo[4:]:
        basis_block(i, j)
    sums = gather_sums(range(NB))

    y_copy(2, 0).wait_recv()
    x_start(2, 1)
    y_copy(2, 1).wait_recv()
    x_start(2, 0)

    for d in (3, 1, 2):
        x_wait(d)
        chain(d)
        combine(d)

    for first in (0, 2):
        new = range(first, first + 2)
        pairs = [(b, k) for k in new for b in range(NB)]
        spots = [((b, NB + k),) for b, k in pairs]
        extra = [(NB + first, first), (NB + first, first + 1), (NB + first + 1, first + 1)]
        if first == 2:
            extra += [(NB + t, k) for t in range(2) for k in new]
        pairs = pairs + extra
        spots = spots + [
            ((t, NB + k), (NB + k, t)) if t != NB + k else ((t, t),) for t, k in extra
        ]
        left = {b: (bas, b) for b in range(NB)}
        left.update({NB + t: (w, t) for t in range(first + 2)})
        products(left, {k: (w, k) for k in new}, pairs, spots)

    wide_row = lax.broadcasted_iota(jnp.int32, (NZ, 128), 0)
    wide_lane = lax.broadcasted_iota(jnp.int32, (NZ, 128), 1)
    sums = jnp.where(wide_row < NB, sums, 0.0)
    sums = jnp.where(wide_lane >= NB, gather_sums(range(NB, NZ)), sums)
    sums = jnp.where(wide_lane < NZ, sums, 0.0)
    packed = jnp.where(
        lane < 32,
        sums[0:8],
        jnp.where(lane < 64, pltpu.roll(sums[8:16], 32, 1), pltpu.roll(sums[16:24], 64, 1)),
    )

    def exchange(phase, value):
        me = mine[phase]
        slots[phase, me] = value

        def copy(to, spot):
            return pltpu.make_async_remote_copy(
                slots.at[phase, me],
                slots.at[phase, spot],
                as_.at[phase, to],
                ar.at[phase, spot],
                device_id=group_peer(phase, to),
                device_id_type=MESH,
            )

        def send(i, carry):
            copy((me + i) % 16, me).start()
            return carry

        def receive(i, carry):
            other = (me + i) % 16
            copy(other, other).wait_recv()
            return carry

        lax.fori_loop(1, 16, send, 0)
        lax.fori_loop(1, 16, receive, 0)
        total = slots[phase, 0]
        for m in range(1, 16):
            total = total + slots[phase, m]

        def sent(i, carry):
            copy((me + i) % 16, me).wait_send()
            return carry

        return total, lambda: lax.fori_loop(1, 16, sent, 0)

    packed, drain0 = exchange(0, packed)
    packed, drain1 = exchange(1, packed)

    packed = packed / TOTAL
    means = jnp.concatenate([packed, pltpu.roll(packed, 96, 1), pltpu.roll(packed, 64, 1)], axis=0)
    column = pltpu.roll(means, 128 - NB, 1)
    proj[...] = column[0:NB, 0:S]
    coefs = jnp.where(jnp.logical_and(wide_row < NB, wide_lane < S), column, 0.0)
    twice = -2.0 * coefs
    for b in range(NB):
        twice = twice + jnp.where(wide_row < NB, means[:, b : b + 1], 0.0) * coefs[b : b + 1]
    gram = []
    for s in range(S):
        row = jnp.sum(coefs[:, s : s + 1] * twice, axis=0, keepdims=True) + column[NB + s : NB + s + 1]
        gram.append([jnp.broadcast_to(row[:, t : t + 1], (8, 128)) for t in range(S)])

    lower = [[None] * S for _ in range(S)]
    inverse = [[None] * S for _ in range(S)]
    for j in range(S):
        value = gram[j][j]
        for k in range(j):
            value = value - lower[j][k] * lower[j][k]
        lower[j][j] = jnp.sqrt(value)
        inverse[j][j] = 1.0 / lower[j][j]
        for i in range(j + 1, S):
            value = gram[i][j]
            for k in range(j):
                value = value - lower[i][k] * lower[j][k]
            lower[i][j] = value * inverse[j][j]
    for j in range(S):
        for i in range(j + 1, S):
            value = lower[i][j] * inverse[j][j]
            for k in range(j + 1, i):
                value = value + lower[i][k] * inverse[k][j]
            inverse[i][j] = -inverse[i][i] * value
    upper_factor = jnp.zeros((8, 128), F32)
    for s in range(S):
        for t in range(s + 1):
            upper_factor = jnp.where(jnp.logical_and(sub == t, lane == s), lower[s][t], upper_factor)
    factor[...] = upper_factor[0:S, 0:S]

    for s in range(S):
        value = None
        for t in range(s + 1):
            term = jnp.broadcast_to(coefs[:, t : t + 1], (NZ, 128)) * inverse[s][t][0:1]
            value = term if value is None else value + term
        cf[s] = -value
        for t in range(s + 1):
            cf[s, NB + t : NB + t + 1] = inverse[s][t][0:1]

    def out_copy(v):
        return pltpu.make_async_copy(w.at[:, v], block.at[:, v], out_sem.at[v])

    def finish(v, carry):
        def weight(s, n):
            return jnp.broadcast_to(cf[s, n : n + 1], (8, 128))

        totals = [[None] * LAYERS for _ in range(S)]
        for n in range(NZ):
            vectors = [(w[n - NB, v, l] if n >= NB else bas[n, v, l]) for l in range(LAYERS)]
            for s in range(S):
                if n >= NB and n - NB > s:
                    continue
                m = weight(s, n)
                for l in range(LAYERS):
                    term = m * vectors[l]
                    totals[s][l] = term if totals[s][l] is None else totals[s][l] + term
        for s in range(S):
            for l in range(LAYERS):
                w[s, v, l] = totals[s][l]
        out_copy(v).start()
        return carry

    lax.fori_loop(0, VARS, finish, 0)

    drain0()
    drain1()
    for d in range(4):
        for h in range(2):
            if d > 0:
                y_copy(d, h).wait_send()

            @pl.when(sends[h])
            def _():
                x_copy(d, h).wait_send()

    for side in range(2):

        @pl.when(sends[side])
        def _():
            for copy in side_copies(side):
                copy.wait_send()

    def landed(v, carry):
        out_copy(v).wait()
        return carry

    lax.fori_loop(0, VARS, landed, 0)


def shards(start, shifted_diag, face_coef, mixing, neighbours, basis):
    view = start.reshape(4, VARS, LAYERS, 2, 128).transpose(1, 2, 3, 0, 4).reshape(VARS, LAYERS, 8, 128)
    vectors = basis.reshape(NB, 4, VARS, LAYERS, 2, 128).transpose(0, 2, 3, 4, 1, 5)
    vectors = vectors.reshape(NB, VARS, LAYERS, 8, 128)
    hbm = pl.BlockSpec(memory_space=pl.ANY)
    vmem = pl.BlockSpec(memory_space=pltpu.VMEM)
    dma = pltpu.SemaphoreType.DMA
    block, proj, factor = pl.pallas_call(
        kernel,
        out_shape=(
            jax.ShapeDtypeStruct((S, VARS, LAYERS, 8, 128), F32),
            jax.ShapeDtypeStruct((NB, S), F32),
            jax.ShapeDtypeStruct((S, S), F32),
        ),
        in_specs=[hbm, hbm, hbm, hbm, hbm, pl.BlockSpec(memory_space=pltpu.SMEM), vmem],
        out_specs=(hbm, vmem, vmem),
        scratch_shapes=[
            pltpu.VMEM((4, 4, VARS, WIDE, 8, 128), F32),
            pltpu.VMEM((VARS, WIDE, 8, 128), F32),
            pltpu.VMEM((S, VARS, LAYERS, 8, 128), F32),
            pltpu.VMEM((NB, VARS, LAYERS, 8, 128), F32),
            pltpu.VMEM((FACES, LAYERS * FACE), F32),
            pltpu.VMEM((FACES, LAYERS * FACE), jnp.int32),
            pltpu.VMEM((16, 128), F32),
            pltpu.VMEM((2, FACES, 3 * FACE), F32),
            pltpu.VMEM((2, FACES, 3 * FACE), jnp.int32),
            pltpu.VMEM((2, 16, 128), F32),
            pltpu.VMEM((8, WIDE, 8, 128), F32),
            pltpu.VMEM((4, WIDE, 8, 128), jnp.int32),
            pltpu.VMEM((VARS * VARS, 8, 128), F32),
            pltpu.VMEM((NZ * NZ * 8, 128), F32),
            pltpu.VMEM((S, NZ, 128), F32),
            pltpu.VMEM((2, 16, 8, 128), F32),
            dma((5,)),
            dma((4, 2)),
            dma((4, 2)),
            dma((4, 2)),
            dma((4, 2)),
            dma((2, 3)),
            dma((2, 3)),
            dma((VARS,)),
            dma((2, 16)),
            dma((2, 16)),
        ],
        compiler_params=pltpu.CompilerParams(
            collective_id=0, has_side_effects=True, vmem_limit_bytes=40 * 1024 * 1024
        ),
        name="krylov_block",
    )(view, face_coef, neighbours, shifted_diag.reshape(16, 128), vectors, mixing, jnp.asarray(time_tables()))
    block = block.reshape(S, VARS, LAYERS, 2, 4, 128).transpose(0, 4, 1, 2, 3, 5)
    return block.reshape(S, 4, VARS, LAYERS * FACE), proj, factor


def solution(mesh):
    return jax.shard_map(
        shards,
        mesh=mesh,
        in_specs=(
            P("inst", None, "space"),
            P("space"),
            P(None, "space"),
            P(),
            P(None, "space"),
            P(None, "inst", None, "space"),
        ),
        out_specs=(P(None, "inst", None, "space"), P(), P()),
        check_vma=False,
    )
```

```python
import math

import jax
import jax.numpy as jnp
import numpy as np
from jax import lax
from jax.experimental import pallas as pl
from jax.experimental.pallas import tpu as pltpu
from jax.sharding import PartitionSpec as P

NT = 16
VARS = 7
NB = 20
S = 4
FACES = 6
FACE = 256
LAYERS = 8
NZ = NB + S
WIDE = 16
MESH = pl.DeviceIdType.MESH
F32 = jnp.float32
BF16 = jnp.bfloat16
UNITS = 14
TOTAL = float(NT * VARS * 131072)


def time_tables():
    n = np.arange(NT)
    diff = n[:, None] - n[None, :]
    angle = np.where(diff == 0, 1.0, np.pi * diff / NT)
    dmat = np.where(diff == 0, 0.0, 0.5 * (-1.0) ** diff * np.cos(angle) / np.sin(angle))
    tables = np.zeros((4, 8 * S, 8 * S))
    for d in range(4):
        for k in range(1, S + 1):
            for j in range(k):
                power = np.linalg.matrix_power(0.1 * dmat, k - j)
                part = math.comb(k, j) * power[:4, 4 * d : 4 * d + 4]
                for half in range(2):
                    r, c = (k - 1) * 8 + half * 4, j * 8 + half * 4
                    tables[d, r : r + 4, c : c + 4] = part
    high = tables.astype(jnp.bfloat16).astype(np.float64)
    low = (tables - high).astype(jnp.bfloat16).astype(np.float64)
    return np.concatenate([high, high, low], axis=2).astype(np.float32)


def kernel(
    start, coef, near, diag, basis, mixing, times,
    krylov, products_out,
    u, u4, w, bas, coef_own, near_own, diag_own, coef_side, near_side, diag_side,
    mixing_own, tables, geo, weights, mix, sums, slots,
    load_sem, ys, yr, xs, xr, gs, gr, as_, ar, out_sem,
):
    p, q = lax.axis_index("space"), lax.axis_index("inst")
    z, x, c = p // 8, (p // 2) % 4, p % 2
    has_low, has_high = p > 0, p < 63
    y_up, y_down = (q + 1) % 4, (q + 3) % 4

    def group_peer(phase, m):
        if phase == 0:
            return {"space": (z * 4 + m // 4) * 2 + c, "inst": m % 4}
        return {"space": ((m // 2) * 4 + x) * 2 + m % 2, "inst": q}

    mine = (x * 4 + q, z * 2 + c)

    loads = [
        pltpu.make_async_copy(coef, coef_own, load_sem.at[0]),
        pltpu.make_async_copy(near, near_own, load_sem.at[1]),
        pltpu.make_async_copy(diag, diag_own, load_sem.at[2]),
        pltpu.make_async_copy(mixing, mixing_own, load_sem.at[3]),
        pltpu.make_async_copy(start, u.at[0, 0, :, pl.ds(4, LAYERS)], load_sem.at[4]),
        pltpu.make_async_copy(times, tables, load_sem.at[5]),
        pltpu.make_async_copy(basis, bas, load_sem.at[6]),
    ]
    for copy in loads:
        copy.start()

    barrier = pltpu.get_barrier_semaphore()

    def greet(phase):
        def body(i, carry):
            pl.semaphore_signal(
                barrier, inc=1, device_id=group_peer(phase, (mine[phase] + i) % 16), device_id_type=MESH
            )
            return carry

        lax.fori_loop(1, 16, body, 0)

    greet(0)
    greet(1)

    @pl.when(has_low)
    def _():
        pl.semaphore_signal(barrier, inc=1, device_id={"space": p - 1, "inst": q}, device_id_type=MESH)

    @pl.when(has_high)
    def _():
        pl.semaphore_signal(barrier, inc=1, device_id={"space": p + 1, "inst": q}, device_id_type=MESH)

    pl.semaphore_wait(barrier, 30 + jnp.where(has_low, 1, 0) + jnp.where(has_high, 1, 0))

    def y_copy(d, h):
        dst = u.at[0, d, :, pl.ds(4 + 4 * h, 4)]
        if d == 2:
            src = u.at[0, 3 if h == 0 else 1, :, pl.ds(4 + 4 * h, 4)]
            to = y_up if h == 0 else y_down
        else:
            src = start.at[:, pl.ds(4 * h, 4)]
            to = y_up if d == 3 else y_down
        return pltpu.make_async_remote_copy(
            src, dst, ys.at[d, h], yr.at[d, h], device_id={"space": p, "inst": to}, device_id_type=MESH
        )

    def x_copy(d, side):
        count = 4 if d == 0 else 3
        if side == 0:
            dst = u.at[0, d, :, pl.ds(4 - count, count)]
            src = start.at[:, pl.ds(8 - count, count)] if d == 0 else u.at[0, d, :, pl.ds(12 - count, count)]
            to = p + 1
        else:
            dst = u.at[0, d, :, pl.ds(12, count)]
            src = start.at[:, pl.ds(0, count)] if d == 0 else u.at[0, d, :, pl.ds(4, count)]
            to = p - 1
        return pltpu.make_async_remote_copy(
            src, dst, xs.at[d, side], xr.at[d, side], device_id={"space": to, "inst": q}, device_id_type=MESH
        )

    def side_copies(side):
        to = p + 1 if side == 0 else p - 1
        cut = pl.ds(5 * FACE, 3 * FACE) if side == 0 else pl.ds(0, 3 * FACE)
        pairs = (
            (coef.at[:, cut], coef_side.at[side]),
            (near.at[:, cut], near_side.at[side]),
            (diag, diag_side.at[side]),
        )
        return [
            pltpu.make_async_remote_copy(
                src, dst, gs.at[side, i], gr.at[side, i], device_id={"space": to, "inst": q}, device_id_type=MESH
            )
            for i, (src, dst) in enumerate(pairs)
        ]

    sends = (has_high, has_low)
    hears = (has_low, has_high)

    def x_start(d, side):
        @pl.when(sends[side])
        def _():
            x_copy(d, side).start()

    y_copy(3, 0).start()
    y_copy(1, 1).start()
    for side in range(2):

        @pl.when(sends[side])
        def _():
            for copy in side_copies(side):
                copy.start()

        x_start(0, side)
    y_copy(3, 1).start()
    y_copy(1, 0).start()

    for side in range(2):

        @pl.when(jnp.logical_not(hears[side]))
        def _():
            coef_side[side] = jnp.zeros((FACES, 3 * FACE), F32)
            near_side[side] = jnp.zeros((FACES, 3 * FACE), jnp.int32)
            diag_side[side] = jnp.zeros((16, 128), F32)
            for d in range(4):
                first = 0 if side == 0 else 12
                u[0, d, :, pl.ds(first, 4)] = jnp.zeros((VARS, 4, 8, 128), F32)

    sub = lax.broadcasted_iota(jnp.int32, (8, 128), 0)
    lane = lax.broadcasted_iota(jnp.int32, (8, 128), 1)
    upper = sub >= 4

    for copy in loads[:4]:
        copy.wait()

    matrix = mixing_own[...]
    for i in range(VARS):
        for j in range(VARS):
            mix[i * VARS + j] = jnp.broadcast_to(matrix[i : i + 1, j : j + 1], (8, 128))

    def spread(values, at):
        first = jnp.broadcast_to(values[:, at : at + 128], (8, 128))
        second = jnp.broadcast_to(values[:, at + 128 : at + 256], (8, 128))
        return jnp.where(upper, second, first)

    source = lax.broadcasted_iota(jnp.int32, (32, FACE), 0)

    def place(layer, coefs, nears, at, diags):
        values = [spread(coefs[f : f + 1], at) for f in range(FACES)]
        geo[0, layer] = sum(values[1:], values[0])
        geo[1, layer], geo[2, layer] = values[0], values[1]
        geo[3, layer] = jnp.where(
            upper, jnp.broadcast_to(diags[1:2], (8, 128)), jnp.broadcast_to(diags[0:1], (8, 128))
        )
        rows = [
            (nears[f : f + 1, at : at + FACE] & (FACE - 1), coefs[f : f + 1, at : at + FACE])
            for f in range(2, FACES)
        ]

        for r in range(0, FACE, 32):
            total = None
            for cells, values in rows:
                term = jnp.where(source + r == cells, values, 0.0)
                total = term if total is None else total + term
            high = total.astype(BF16)
            weights[layer, 0, pl.ds(r, 32)] = high
            weights[layer, 1, pl.ds(r, 32)] = (total - high.astype(F32)).astype(BF16)

    coefs, nears, diags = coef_own[...], near_own[...], diag_own[...]
    for layer in range(LAYERS):
        place(4 + layer, coefs, nears, layer * FACE, diags[2 * layer : 2 * layer + 2])
    for side in range(2):

        @pl.when(hears[side])
        def _():
            for copy in side_copies(side):
                copy.wait_recv()

        coefs, nears, diags = coef_side[side], near_side[side], diag_side[side]
        for layer in range(3):
            first = 10 + 2 * layer if side == 0 else 2 * layer
            place((1 if side == 0 else 12) + layer, coefs, nears, layer * FACE, diags[first : first + 2])

    def within(groups, layer):
        rows = []
        for values in groups:
            for i in range(0, VARS, 2):
                one = values[i]
                two = values[min(i + 1, VARS - 1)]
                first = jnp.where(upper, pltpu.roll(two, 4, 0), one)
                second = jnp.where(upper, two, pltpu.roll(one, 4, 0))
                rows.append(jnp.concatenate([first, second], axis=1))
        rows = jnp.concatenate(rows, axis=0)
        count = rows.shape[0]
        high = rows.astype(BF16)
        low = (rows - high.astype(F32)).astype(BF16)
        both = jnp.dot(jnp.concatenate([high, low], axis=0), weights[layer, 0], preferred_element_type=F32)
        out = both[0:count] + both[count:] + jnp.dot(high, weights[layer, 1], preferred_element_type=F32)
        results = []
        for at in range(0, count, 32):
            result = []
            for i in range(0, VARS, 2):
                first, second = (out[at + 4 * i : at + 4 * i + 8, e : e + 128] for e in (0, 128))
                if i + 1 == VARS:
                    result.append(jnp.where(upper, second, first))
                else:
                    result.append(jnp.where(upper, pltpu.roll(second, 4, 0), first))
                    result.append(jnp.where(upper, second, pltpu.roll(first, 4, 0)))
            results.append(result)
        return results

    def step(pairs, low, high):
        count = max(n for n in range(1, UNITS // len(pairs) + 1) if (high - low) % n == 0)

        def body(i, carry):
            layers = [low + count * i + e for e in range(count)]
            fluxes = []
            for b in layers:
                centers = [[src[v, b] for v in range(VARS)] for src, _ in pairs]
                inner = within(centers, b)
                g = [geo[f, b] for f in range(3)]
                for (src, _), center, inside in zip(pairs, centers, inner):
                    fluxes.append(
                        [
                            g[0] * center[v] - g[1] * src[v, b - 1] - g[2] * src[v, b + 1] - inside[v]
                            for v in range(VARS)
                        ]
                    )
            units = [(src, dst, b) for b in layers for src, dst in pairs]
            for i in range(VARS):
                totals = [geo[3, b] * src[i, b] for src, _, b in units]
                for j in range(VARS):
                    m = mix[i * VARS + j]
                    totals = [t + m * flux[j] for t, flux in zip(totals, fluxes)]
                for (_, dst, b), total in zip(units, totals):
                    dst[i, b] = total
            return carry

        lax.fori_loop(0, (high - low) // count, body, 0)

    def chain(*groups):
        low = 1 if groups[0] == 0 else 2
        for j in range(3):
            step([(u.at[j, d], u.at[j + 1, d]) for d in groups], low + j, 16 - low - j)
        if groups[0] == 0:
            step([(u.at[3, 0], u4)], 4, 12)

    def combine(*groups):
        table = jnp.concatenate([tables[d] for d in groups], axis=1).astype(BF16)
        for v in range(VARS):
            stack = []
            for d in groups:
                parts = jnp.concatenate(
                    [jnp.concatenate([u[j, d, v, 4 + l] for l in range(LAYERS)], axis=1) for j in range(S)],
                    axis=0,
                )
                high = parts.astype(BF16)
                low = (parts - high.astype(F32)).astype(BF16)
                stack += [high, low, high]
            out = jnp.dot(table, jnp.concatenate(stack, axis=0), preferred_element_type=F32)
            for l in range(LAYERS):
                for k in range(S):
                    term = out[8 * k : 8 * k + 8, 128 * l : 128 * l + 128]
                    if groups[0] == 0:
                        last = u4[v, 4 + l] if k == S - 1 else u[k + 1, 0, v, 4 + l]
                        w[k, v, l] = last + term
                    else:
                        w[k, v, l] += term

    bits = {k: (sub // k) % 2 == 1 for k in (1, 2, 4)}
    zero = jnp.zeros((8, 128), F32)

    def merge(parts):
        for k in (1, 2, 4):
            parts = [
                jnp.where(bits[k], b, a) + pltpu.roll(jnp.where(bits[k], a, b), k, 0)
                for a, b in zip(parts[::2], parts[1::2])
            ]
        return parts[0]

    def products(left, right, pairs):
        def body(v, totals):
            totals = list(totals)
            for l in range(LAYERS):
                a = {k: r[n, v, l] for k, (r, n) in left.items()}
                b = {k: r[n, v, l] for k, (r, n) in right.items()}
                totals = [t + a[m] * b[n] for t, (m, n) in zip(totals, pairs)]
            return tuple(totals)

        totals = lax.fori_loop(0, VARS, body, (zero,) * len(pairs))
        return dict(zip(pairs, totals))

    def basis_block(i, j):
        rows = range(8 * i, min(8 * i + 8, NB))
        columns = range(5 * j, 5 * j + 5)
        totals = products(
            {a: (bas, a) for a in rows},
            {b: (bas, b) for b in columns},
            [(a, b) for a in rows for b in columns if a <= b],
        )
        for b in columns:
            sums[b, pl.ds(8 * i, 8)] = merge([totals.get((a, b), zero) for a in range(8 * i, 8 * i + 8)])

    wide_row = lax.broadcasted_iota(jnp.int32, (NZ, 128), 0)
    wide_lane = lax.broadcasted_iota(jnp.int32, (NZ, 128), 1)

    def merge_lanes(columns):
        parts = [columns.get(i) for i in range(32)]
        for k in (1, 2, 4, 8, 16):
            bit = (lane // k) % 2 == 1
            merged = []
            for a, b in zip(parts[::2], parts[1::2]):
                if a is None and b is None:
                    merged.append(None)
                    continue
                a, b = zero if a is None else a, zero if b is None else b
                merged.append(jnp.where(bit, b, a) + pltpu.roll(jnp.where(bit, a, b), k, 1))
            parts = merged
        total = parts[0]
        total = total + pltpu.roll(total, 32, 1)
        return total + pltpu.roll(total, 64, 1)

    column_of = lane % 32

    def basis_sums():
        result = []
        for i in range(3):
            part = merge_lanes({b: sums[b, pl.ds(8 * i, 8)] for b in range(8 * i, NB)})
            part = jnp.where(sub + 8 * i <= column_of, part, 0.0)
            part = jnp.where(sub + 8 * i == column_of, 0.5 * part, part)
            result.append(jnp.where(column_of < NB, part, 0.0))
        return result

    def x_wait(d):
        for side in range(2):

            @pl.when(hears[side])
            def _():
                x_copy(d, side).wait_recv()

    loads[4].wait()
    loads[5].wait()
    x_wait(0)
    chain(0)
    combine(0)

    y_copy(3, 0).wait_recv()
    y_copy(2, 0).start()
    y_copy(1, 1).wait_recv()
    y_copy(2, 1).start()
    x_start(3, 1)
    x_start(1, 0)

    loads[6].wait()
    for i, j in ((0, 0), (0, 1), (0, 2)):
        basis_block(i, j)

    y_copy(3, 1).wait_recv()
    x_start(3, 0)
    y_copy(1, 0).wait_recv()
    x_start(1, 1)

    for i, j in ((0, 3), (1, 1), (1, 2), (1, 3), (2, 3)):
        basis_block(i, j)
    known = basis_sums()

    y_copy(2, 0).wait_recv()
    x_start(2, 1)
    y_copy(2, 1).wait_recv()
    x_start(2, 0)

    x_wait(3)
    x_wait(1)
    chain(3, 1)
    combine(3, 1)
    x_wait(2)
    chain(2)
    combine(2)

    krylov_copy = pltpu.make_async_copy(w, krylov, out_sem.at[0])
    krylov_copy.start()

    fresh = {}
    for first in (0, 2):
        new = range(first, first + 2)
        pairs = [(b, k) for k in new for b in range(NB)]
        pairs += [(NB + t, k) for k in new for t in range(k + 1)]
        left = {b: (bas, b) for b in range(NB)}
        left.update({NB + t: (w, t) for t in range(first + 2)})
        totals = products(left, {k: (w, k) for k in new}, pairs)
        for t, k in pairs:
            if t >= NB:
                totals[NB + k, t - NB] = totals[t, k]
        fresh.update(totals)
        for k in new:
            for i in range(2):
                sums[NB + k, pl.ds(8 * i, 8)] = merge([fresh[b, k] for b in range(8 * i, 8 * i + 8)])
    for k in range(S):
        sums[NB + k, pl.ds(16, 8)] = merge([fresh[b, k] for b in range(16, 24)])
    total = []
    for i in range(3):
        fresh_part = merge_lanes({NB + k: sums[NB + k, pl.ds(8 * i, 8)] for k in range(S)})
        total.append(jnp.where(column_of < NB, known[i], fresh_part))
    packed = jnp.where(lane < 32, total[0], jnp.where(lane < 64, total[1], total[2]))

    def exchange(phase, value):
        me = mine[phase]
        slots[phase, me] = value

        def copy(to, spot):
            return pltpu.make_async_remote_copy(
                slots.at[phase, me],
                slots.at[phase, spot],
                as_.at[phase, to],
                ar.at[phase, spot],
                device_id=group_peer(phase, to),
                device_id_type=MESH,
            )

        def send(i, carry):
            copy((me + i) % 16, me).start()
            return carry

        def receive(i, carry):
            other = (me + i) % 16
            copy(other, other).wait_recv()
            return carry

        lax.fori_loop(1, 16, send, 0)
        lax.fori_loop(1, 16, receive, 0)
        total = slots[phase, 0]
        for m in range(1, 16):
            total = total + slots[phase, m]

        def sent(i, carry):
            copy((me + i) % 16, me).wait_send()
            return carry

        return total, lambda: lax.fori_loop(1, 16, sent, 0)

    packed, drain0 = exchange(0, packed)
    packed, drain1 = exchange(1, packed)

    products_out[...] = packed

    drain0()
    drain1()
    for d in range(4):
        for h in range(2):
            if d > 0:
                y_copy(d, h).wait_send()

            @pl.when(sends[h])
            def _():
                x_copy(d, h).wait_send()

    for side in range(2):

        @pl.when(sends[side])
        def _():
            for copy in side_copies(side):
                copy.wait_send()
    krylov_copy.wait()


def normalize(packed_ref, krylov, basis, block, proj, factor, w, bas, cf, in_sem, out_sem):
    def arrive(v):
        return (
            pltpu.make_async_copy(basis.at[:, v], bas.at[:, v], in_sem.at[0, v]),
            pltpu.make_async_copy(krylov.at[:, v], w.at[:, v], in_sem.at[1, v]),
        )

    def leave(v):
        return pltpu.make_async_copy(w.at[:, v], block.at[:, v], out_sem.at[v])

    for v in range(VARS):
        for copy in arrive(v):
            copy.start()

    sub = lax.broadcasted_iota(jnp.int32, (8, 128), 0)
    lane = lax.broadcasted_iota(jnp.int32, (8, 128), 1)
    wide_row = lax.broadcasted_iota(jnp.int32, (NZ, 128), 0)
    wide_lane = lax.broadcasted_iota(jnp.int32, (NZ, 128), 1)
    packed = packed_ref[...] / TOTAL
    means = jnp.concatenate([packed, pltpu.roll(packed, 96, 1), pltpu.roll(packed, 64, 1)], axis=0)
    column = pltpu.roll(means, 128 - NB, 1)
    proj[...] = jnp.concatenate([column, jnp.zeros((128 - NZ, 128), F32)], axis=0).T[0:S, 0:NB]
    coefs = jnp.where(jnp.logical_and(wide_row < NB, wide_lane < S), column, 0.0)
    half = jnp.where(jnp.logical_and(wide_row < NB, wide_lane < NB), means, 0.0)
    rest = -coefs
    for b in range(NB):
        rest = rest + half[:, b : b + 1] * coefs[b : b + 1]
    cross = [jnp.sum(coefs[:, s : s + 1] * rest, axis=0, keepdims=True) for s in range(S)]
    gram = [[None] * S for _ in range(S)]
    for s in range(S):
        for t in range(s + 1):
            value = column[NB + s : NB + s + 1, t : t + 1] + cross[s][:, t : t + 1] + cross[t][:, s : s + 1]
            gram[s][t] = jnp.broadcast_to(value, (8, 128))

    lower = [[None] * S for _ in range(S)]
    inverse = [[None] * S for _ in range(S)]
    for j in range(S):
        value = gram[j][j]
        for k in range(j):
            value = value - lower[j][k] * lower[j][k]
        lower[j][j] = jnp.sqrt(value)
        inverse[j][j] = 1.0 / lower[j][j]
        for i in range(j + 1, S):
            value = gram[i][j]
            for k in range(j):
                value = value - lower[i][k] * lower[j][k]
            lower[i][j] = value * inverse[j][j]
    for j in range(S):
        for i in range(j + 1, S):
            value = lower[i][j] * inverse[j][j]
            for k in range(j + 1, i):
                value = value + lower[i][k] * inverse[k][j]
            inverse[i][j] = -inverse[i][i] * value
    upper_factor = jnp.zeros((8, 128), F32)
    for s in range(S):
        for t in range(s + 1):
            upper_factor = jnp.where(jnp.logical_and(sub == t, lane == s), lower[s][t], upper_factor)
    factor[...] = upper_factor[0:S, 0:S]

    for s in range(S):
        value = None
        for t in range(s + 1):
            term = jnp.broadcast_to(coefs[:, t : t + 1], (NZ, 128)) * inverse[s][t][0:1]
            value = term if value is None else value + term
        cf[s] = -value
        for t in range(s + 1):
            cf[s, NB + t : NB + t + 1] = inverse[s][t][0:1]

    def finish(v, carry):
        for copy in arrive(v):
            copy.wait()

        def weight(s, n):
            return jnp.broadcast_to(cf[s, n : n + 1], (8, 128))

        totals = [[None] * LAYERS for _ in range(S)]
        for n in range(NZ):
            vectors = [(w[n - NB, v, l] if n >= NB else bas[n, v, l]) for l in range(LAYERS)]
            for s in range(S):
                if n >= NB and n - NB > s:
                    continue
                m = weight(s, n)
                for l in range(LAYERS):
                    term = m * vectors[l]
                    totals[s][l] = term if totals[s][l] is None else totals[s][l] + term
        for s in range(S):
            for l in range(LAYERS):
                w[s, v, l] = totals[s][l]
        leave(v).start()
        return carry

    lax.fori_loop(0, VARS, finish, 0)

    for v in range(VARS):
        leave(v).wait()


def shards(start, shifted_diag, face_coef, mixing, neighbours, basis):
    view = start.reshape(4, VARS, LAYERS, 2, 128).transpose(1, 2, 3, 0, 4).reshape(VARS, LAYERS, 8, 128)
    vectors = basis.reshape(NB, 4, VARS, LAYERS, 2, 128).transpose(0, 2, 3, 4, 1, 5)
    vectors = vectors.reshape(NB, VARS, LAYERS, 8, 128)
    hbm = pl.BlockSpec(memory_space=pltpu.HBM)
    vmem = pl.BlockSpec(memory_space=pltpu.VMEM)
    dma = pltpu.SemaphoreType.DMA
    krylov, packed = pl.pallas_call(
        kernel,
        out_shape=(
            jax.ShapeDtypeStruct((S, VARS, LAYERS, 8, 128), F32),
            jax.ShapeDtypeStruct((8, 128), F32),
        ),
        in_specs=[hbm] * 7,
        out_specs=(hbm, vmem),
        scratch_shapes=[
            pltpu.VMEM((4, 4, VARS, WIDE, 8, 128), F32),
            pltpu.VMEM((VARS, WIDE, 8, 128), F32),
            pltpu.VMEM((S, VARS, LAYERS, 8, 128), F32),
            pltpu.VMEM((NB, VARS, LAYERS, 8, 128), F32),
            pltpu.VMEM((FACES, LAYERS * FACE), F32),
            pltpu.VMEM((FACES, LAYERS * FACE), jnp.int32),
            pltpu.VMEM((16, 128), F32),
            pltpu.VMEM((2, FACES, 3 * FACE), F32),
            pltpu.VMEM((2, FACES, 3 * FACE), jnp.int32),
            pltpu.VMEM((2, 16, 128), F32),
            pltpu.VMEM((VARS, VARS), F32),
            pltpu.VMEM((4, 8 * S, 24 * S), F32),
            pltpu.VMEM((4, WIDE, 8, 128), F32),
            pltpu.VMEM((WIDE, 2, FACE, FACE), BF16),
            pltpu.VMEM((VARS * VARS, 8, 128), F32),
            pltpu.VMEM((NZ, NZ, 128), F32),
            pltpu.VMEM((2, 16, 8, 128), F32),
            dma((7,)),
            dma((4, 2)),
            dma((4, 2)),
            dma((4, 2)),
            dma((4, 2)),
            dma((2, 3)),
            dma((2, 3)),
            dma((2, 16)),
            dma((2, 16)),
            dma((1,)),
        ],
        compiler_params=pltpu.CompilerParams(
            collective_id=0, has_side_effects=True, vmem_limit_bytes=56 * 1024 * 1024
        ),
        name="krylov_block",
    )(view, face_coef, neighbours, shifted_diag.reshape(16, 128), vectors, mixing, jnp.asarray(time_tables()))
    block, proj, factor = pl.pallas_call(
        normalize,
        out_shape=(
            jax.ShapeDtypeStruct((S, VARS, LAYERS, 8, 128), F32),
            jax.ShapeDtypeStruct((S, NB), F32),
            jax.ShapeDtypeStruct((S, S), F32),
        ),
        in_specs=[vmem, hbm, hbm],
        out_specs=(hbm, vmem, vmem),
        scratch_shapes=[
            pltpu.VMEM((S, VARS, LAYERS, 8, 128), F32),
            pltpu.VMEM((NB, VARS, LAYERS, 8, 128), F32),
            pltpu.VMEM((S, NZ, 128), F32),
            dma((2, VARS)),
            dma((VARS,)),
        ],
        compiler_params=pltpu.CompilerParams(vmem_limit_bytes=56 * 1024 * 1024),
        name="normalize",
    )(packed, krylov, vectors)
    block = block.reshape(S, VARS, LAYERS, 2, 4, 128).transpose(0, 4, 1, 2, 3, 5)
    return block.reshape(S, 4, VARS, LAYERS * FACE), proj.T, factor


def solution(mesh):
    return jax.shard_map(
        shards,
        mesh=mesh,
        in_specs=(
            P("inst", None, "space"),
            P("space"),
            P(None, "space"),
            P(),
            P(None, "space"),
            P(None, "inst", None, "space"),
        ),
        out_specs=(P(None, "inst", None, "space"), P(), P()),
        check_vma=False,
    )
```

```python
import math

import jax
import jax.numpy as jnp
import numpy as np
from jax import lax
from jax.experimental import pallas as pl
from jax.experimental.pallas import tpu as pltpu
from jax.sharding import PartitionSpec as P

NT = 16
VARS = 7
NB = 20
S = 4
FACES = 6
FACE = 256
LAYERS = 8
NZ = NB + S
WIDE = 16
MESH = pl.DeviceIdType.MESH
F32 = jnp.float32
BF16 = jnp.bfloat16
TOTAL = float(NT * VARS * 131072)


GATHER = lax.GatherDimensionNumbers(
    offset_dims=(),
    collapsed_slice_dims=(1,),
    start_index_map=(1,),
    operand_batching_dims=(0,),
    start_indices_batching_dims=(0,),
)


def time_tables():
    n = np.arange(NT)
    diff = n[:, None] - n[None, :]
    angle = np.where(diff == 0, 1.0, np.pi * diff / NT)
    dmat = np.where(diff == 0, 0.0, 0.5 * (-1.0) ** diff * np.cos(angle) / np.sin(angle))
    tables = np.zeros((4, 8 * S, 8 * S))
    for d in range(4):
        for k in range(1, S + 1):
            for j in range(k):
                power = np.linalg.matrix_power(0.1 * dmat, k - j)
                part = math.comb(k, j) * power[:4, 4 * d : 4 * d + 4]
                for half in range(2):
                    r, c = (k - 1) * 8 + half * 4, j * 8 + half * 4
                    tables[d, r : r + 4, c : c + 4] = part
    high = tables.astype(jnp.bfloat16).astype(np.float64)
    low = (tables - high).astype(jnp.bfloat16).astype(np.float64)
    return np.concatenate([high, high, low], axis=2).astype(np.float32)


def basis_parts():
    blocks = {}
    for a in range(NB):
        for b in range(a, NB):
            blocks.setdefault((a // 8, b // 5), []).append((a, b))
    blocks[1, 1] += blocks.pop((2, 3))
    parts, at = [], 0
    for pairs in blocks.values():
        parts.append((pairs, at))
        at += -(-len(pairs) // 16)
    return parts


PARTS = basis_parts()


def pair_table():
    table = np.zeros((2, 256), np.int32)
    for pairs, at in PARTS:
        for i, pair in enumerate(pairs):
            table[:, 16 * at + i] = pair
    return table.reshape(4, 128)


def take(x, index):
    return lax.gather(
        x, index[:, :, None], GATHER, slice_sizes=(1, 1), mode=lax.GatherScatterMode.PROMISE_IN_BOUNDS
    )


def kernel(
    start, coef, near, diag, basis, mixing, times,
    krylov, products_out,
    u, u4, w, bas, coef_own, near_own, diag_own, coef_side, near_side, diag_side,
    mixing_own, tables, geo, weights, mix, sums, slots, planes,
    load_sem, ys, yr, xs, xr, gs, gr, sum_sem, out_sem,
):
    p, q = lax.axis_index("space"), lax.axis_index("inst")
    z, x, c = p // 8, (p // 2) % 4, p % 2
    has_low, has_high = p > 0, p < 63
    y_up, y_down = (q + 1) % 4, (q + 3) % 4

    def chip(dz, dx, dy, core):
        return {"space": ((z + dz) % 8 * 4 + (x + dx) % 4) * 2 + core, "inst": (q + dy) % 4}

    plane = [(0, dx, dy) for dx in range(4) for dy in range(4)]
    column = [(dz, 0, 0) for dz in range(8)]

    loads = [
        pltpu.make_async_copy(coef, coef_own, load_sem.at[0]),
        pltpu.make_async_copy(near, near_own, load_sem.at[1]),
        pltpu.make_async_copy(diag, diag_own, load_sem.at[2]),
        pltpu.make_async_copy(mixing, mixing_own, load_sem.at[3]),
        pltpu.make_async_copy(start, u.at[0, 0, :, pl.ds(4, LAYERS)], load_sem.at[4]),
        pltpu.make_async_copy(times, tables, load_sem.at[5]),
        pltpu.make_async_copy(basis, bas, load_sem.at[6]),
    ]
    for copy in loads:
        copy.start()

    barrier = pltpu.get_barrier_semaphore()

    def greet(to):
        pl.semaphore_signal(barrier, inc=1, device_id=to, device_id_type=MESH)

    @pl.when(c == 0)
    def _():
        for at in column[1:]:
            greet(chip(*at, 0))
        for at in plane[1:]:
            greet(chip(*at, 0))
        for at in plane:
            greet(chip(*at, 1))

        @pl.when(jnp.logical_and(x == 0, z > 0))
        def _():
            greet({"space": p - 1, "inst": q})

    @pl.when(c == 1)
    def _():
        for at in column:
            greet(chip(*at, 0))
        greet({"space": p, "inst": y_up})
        greet({"space": p, "inst": y_down})

        @pl.when(has_high)
        def _():
            greet({"space": p + 1, "inst": q})

    def y_copy(d, h):
        dst = u.at[0, d, :, pl.ds(4 + 4 * h, 4)]
        if d == 2:
            src = u.at[0, 3 if h == 0 else 1, :, pl.ds(4 + 4 * h, 4)]
            to = y_up if h == 0 else y_down
        else:
            src = start.at[:, pl.ds(4 * h, 4)]
            to = y_up if d == 3 else y_down
        return pltpu.make_async_remote_copy(
            src, dst, ys.at[d, h], yr.at[d, h], device_id={"space": p, "inst": to}, device_id_type=MESH
        )

    def x_copy(d, side):
        count = 4 if d == 0 else 3
        if side == 0:
            dst = u.at[0, d, :, pl.ds(4 - count, count)]
            src = start.at[:, pl.ds(8 - count, count)] if d == 0 else u.at[0, d, :, pl.ds(12 - count, count)]
            to = p + 1
        else:
            dst = u.at[0, d, :, pl.ds(12, count)]
            src = start.at[:, pl.ds(0, count)] if d == 0 else u.at[0, d, :, pl.ds(4, count)]
            to = p - 1
        return pltpu.make_async_remote_copy(
            src, dst, xs.at[d, side], xr.at[d, side], device_id={"space": to, "inst": q}, device_id_type=MESH
        )

    def side_copies(side):
        to = p + 1 if side == 0 else p - 1
        cut = pl.ds(5 * FACE, 3 * FACE) if side == 0 else pl.ds(0, 3 * FACE)
        pairs = (
            (coef.at[:, cut], coef_side.at[side]),
            (near.at[:, cut], near_side.at[side]),
            (diag, diag_side.at[side]),
        )
        return [
            pltpu.make_async_remote_copy(
                src, dst, gs.at[side, i], gr.at[side, i], device_id={"space": to, "inst": q}, device_id_type=MESH
            )
            for i, (src, dst) in enumerate(pairs)
        ]

    sends = (has_high, has_low)
    hears = (has_low, has_high)

    def x_start(d, side):
        @pl.when(sends[side])
        def _():
            x_copy(d, side).start()

    sub = lax.broadcasted_iota(jnp.int32, (8, 128), 0)
    lane = lax.broadcasted_iota(jnp.int32, (8, 128), 1)
    upper = sub >= 4

    for copy in loads[:4]:
        copy.wait()

    matrix = mixing_own[...]
    for i in range(VARS):
        for j in range(VARS):
            mix[i * VARS + j] = jnp.broadcast_to(matrix[i : i + 1, j : j + 1], (8, 128))

    def spread(values, at):
        first = jnp.broadcast_to(values[:, at : at + 128], (8, 128))
        second = jnp.broadcast_to(values[:, at + 128 : at + 256], (8, 128))
        return jnp.where(upper, second, first)

    source = lax.broadcasted_iota(jnp.int32, (32, FACE), 0)

    def place(layer, coefs, nears, at, diags):
        values = [spread(coefs[f : f + 1], at) for f in range(FACES)]
        geo[0, layer] = sum(values[1:], values[0])
        geo[1, layer], geo[2, layer] = values[0], values[1]
        geo[3, layer] = jnp.where(
            upper, jnp.broadcast_to(diags[1:2], (8, 128)), jnp.broadcast_to(diags[0:1], (8, 128))
        )
        rows = [
            (nears[f : f + 1, at : at + FACE] & (FACE - 1), coefs[f : f + 1, at : at + FACE])
            for f in range(2, FACES)
        ]

        for r in range(0, FACE, 32):
            total = None
            for cells, values in rows:
                term = jnp.where(source + r == cells, values, 0.0)
                total = term if total is None else total + term
            high = total.astype(BF16)
            weights[layer, 0, pl.ds(r, 32)] = high
            weights[layer, 1, pl.ds(r, 32)] = (total - high.astype(F32)).astype(BF16)

    coefs, nears, diags = coef_own[...], near_own[...], diag_own[...]
    for layer in range(LAYERS):
        place(4 + layer, coefs, nears, layer * FACE, diags[2 * layer : 2 * layer + 2])
    def within(groups, layer):
        rows = []
        for values in groups:
            for i in range(0, VARS, 2):
                one = values[i]
                two = values[min(i + 1, VARS - 1)]
                first = jnp.where(upper, pltpu.roll(two, 4, 0), one)
                second = jnp.where(upper, two, pltpu.roll(one, 4, 0))
                rows.append(jnp.concatenate([first, second], axis=1))
        rows = jnp.concatenate(rows, axis=0)
        count = rows.shape[0]
        high = rows.astype(BF16)
        low = (rows - high.astype(F32)).astype(BF16)
        both = jnp.dot(jnp.concatenate([high, low], axis=0), weights[layer, 0], preferred_element_type=F32)
        out = both[0:count] + both[count:] + jnp.dot(high, weights[layer, 1], preferred_element_type=F32)
        results = []
        for at in range(0, count, 32):
            result = []
            for i in range(0, VARS, 2):
                first, second = (out[at + 4 * i : at + 4 * i + 8, e : e + 128] for e in (0, 128))
                if i + 1 == VARS:
                    result.append(jnp.where(upper, second, first))
                else:
                    result.append(jnp.where(upper, pltpu.roll(second, 4, 0), first))
                    result.append(jnp.where(upper, second, pltpu.roll(first, 4, 0)))
            results.append(result)
        return results

    def step(groups, j, layers):
        pairs = [(u.at[j, d], u4 if j == 3 else u.at[j + 1, d]) for d in groups]
        fluxes = []
        for b in layers:
            centers = [[src[v, b] for v in range(VARS)] for src, _ in pairs]
            inner = within(centers, b)
            g = [geo[f, b] for f in range(3)]
            for (src, _), center, inside in zip(pairs, centers, inner):
                fluxes.append(
                    [
                        g[0] * center[v] - g[1] * src[v, b - 1] - g[2] * src[v, b + 1] - inside[v]
                        for v in range(VARS)
                    ]
                )
        units = [(src, dst, b) for b in layers for src, dst in pairs]
        for i in range(VARS):
            totals = [geo[3, b] * src[i, b] for src, _, b in units]
            for n in range(VARS):
                m = mix[i * VARS + n]
                totals = [t + m * flux[n] for t, flux in zip(totals, fluxes)]
            for (_, dst, b), total in zip(units, totals):
                dst[i, b] = total

    def inside(*groups):
        for j in range(3):
            step(groups, j, range(5 + j, 11 - j))

    def outside(groups, j):
        reach = (4 if groups[0] == 0 else 3) - j
        step(groups, j, [*range(5 - reach, 5 + j), *range(11 - j, 11 + reach)])

    def combine(*groups):
        table = jnp.concatenate([tables[d] for d in groups], axis=1).astype(BF16)
        for v in range(VARS):
            stack = []
            for d in groups:
                parts = jnp.concatenate(
                    [jnp.concatenate([u[j, d, v, 4 + l] for l in range(LAYERS)], axis=1) for j in range(S)],
                    axis=0,
                )
                high = parts.astype(BF16)
                low = (parts - high.astype(F32)).astype(BF16)
                stack += [high, low, high]
            out = jnp.dot(table, jnp.concatenate(stack, axis=0), preferred_element_type=F32)
            for l in range(LAYERS):
                for k in range(S):
                    term = out[8 * k : 8 * k + 8, 128 * l : 128 * l + 128]
                    if groups[0] == 0:
                        last = u4[v, 4 + l] if k == S - 1 else u[k + 1, 0, v, 4 + l]
                        w[k, v, l] = last + term
                    else:
                        w[k, v, l] += term

    zero = jnp.zeros((8, 128), F32)

    def merge(parts, first=1, last=64):
        k = first
        while k <= last:
            bit = (lane // k) % 2 == 1
            merged = []
            for a, b in zip(parts[::2], parts[1::2]):
                if a is None and b is None:
                    merged.append(None)
                    continue
                a, b = zero if a is None else a, zero if b is None else b
                merged.append(jnp.where(bit, b, a) + pltpu.roll(jnp.where(bit, a, b), k, 1))
            parts, k = merged, 2 * k
        return parts[0]

    def sixteens(values, at):
        for i in range(0, len(values), 16):
            group = values[i : i + 16]
            sums[at + i // 16] = merge(group + [None] * (16 - len(group)), last=8)

    def row(at, count):
        total = merge([sums[at + i] for i in range(count)] + [None] * (8 - count), first=16)
        for k in (4, 2, 1):
            total = total + pltpu.roll(total, k, 0)
        return total

    def products(left, right, pairs):
        def body(v, totals):
            totals = list(totals)
            for l in range(LAYERS):
                a = {k: r[n, v, l] for k, (r, n) in left.items()}
                b = {k: r[n, v, l] for k, (r, n) in right.items()}
                totals = [t + a[m] * b[n] for t, (m, n) in zip(totals, pairs)]
            return tuple(totals)

        totals = lax.fori_loop(0, VARS, body, (zero,) * len(pairs))
        return dict(zip(pairs, totals))

    def basis_part(i):
        pairs, at = PARTS[i]
        totals = products(
            {a: (bas, a) for a, _ in pairs},
            {b: (bas, b) for _, b in pairs},
            pairs,
        )
        sixteens([(0.5 if a == b else 1.0) * totals[a, b] for a, b in pairs], at)

    def x_wait(d):
        for side in range(2):

            @pl.when(hears[side])
            def _():
                x_copy(d, side).wait_recv()

    loads[6].wait()
    for i in range(2):
        basis_part(i)

    @pl.when(c == 0)
    def _():
        pl.semaphore_wait(barrier, 30 + jnp.where(has_low, 1, 0))

    @pl.when(c == 1)
    def _():
        pl.semaphore_wait(barrier, 18 + jnp.where(jnp.logical_and(x == 3, z < 7), 1, 0))

    y_copy(3, 0).start()
    y_copy(1, 1).start()
    for side in range(2):

        @pl.when(sends[side])
        def _():
            for copy in side_copies(side):
                copy.start()

        x_start(0, side)
    y_copy(3, 1).start()
    y_copy(1, 0).start()

    for side in range(2):

        @pl.when(jnp.logical_not(hears[side]))
        def _():
            coef_side[side] = jnp.zeros((FACES, 3 * FACE), F32)
            near_side[side] = jnp.zeros((FACES, 3 * FACE), jnp.int32)
            diag_side[side] = jnp.zeros((16, 128), F32)
            for d in range(4):
                first = 0 if side == 0 else 12
                u[0, d, :, pl.ds(first, 4)] = jnp.zeros((VARS, 4, 8, 128), F32)

    for i in range(2, len(PARTS)):
        basis_part(i)
    known = (row(0, 8), row(8, 8))
    loads[4].wait()
    loads[5].wait()
    inside(0)

    for side in range(2):

        @pl.when(hears[side])
        def _():
            for copy in side_copies(side):
                copy.wait_recv()

        coefs, nears, diags = coef_side[side], near_side[side], diag_side[side]
        for layer in range(3):
            first = 10 + 2 * layer if side == 0 else 2 * layer
            place((1 if side == 0 else 12) + layer, coefs, nears, layer * FACE, diags[first : first + 2])

    y_copy(3, 0).wait_recv()
    y_copy(2, 0).start()
    y_copy(1, 1).wait_recv()
    y_copy(2, 1).start()
    x_start(3, 1)
    x_start(1, 0)

    x_wait(0)
    outside((0,), 0)
    outside((0,), 1)

    y_copy(3, 1).wait_recv()
    x_start(3, 0)
    y_copy(1, 0).wait_recv()
    x_start(1, 1)

    outside((0,), 2)
    step((0,), 3, range(4, 12))
    combine(0)

    y_copy(2, 0).wait_recv()
    x_start(2, 1)
    y_copy(2, 1).wait_recv()
    x_start(2, 0)

    inside(3, 1)
    inside(2)

    x_wait(3)
    x_wait(1)
    for j in range(3):
        outside((3, 1), j)
    combine(3, 1)
    x_wait(2)
    for j in range(3):
        outside((2,), j)
    combine(2)
    krylov_copy = pltpu.make_async_copy(w, krylov, out_sem.at[0])
    krylov_copy.start()

    for first in (0, 2):
        new = range(first, first + 2)
        pairs = [(b, k) for k in new for b in range(NB)]
        pairs += [(NB + t, k) for k in new for t in range(k + 1)]
        left = {b: (bas, b) for b in range(NB)}
        left.update({NB + t: (w, t) for t in range(first + 2)})
        totals = products(left, {k: (w, k) for k in new}, pairs)
        sixteens([totals.get((b, k)) for k in new for b in range(NZ)], 16 + 3 * (first // 2))
    packed = jnp.where(sub == 0, row(16, 6), jnp.where(sub == 1, known[0], known[1]))[0:4]

    def plane_copy(at, spot):
        return pltpu.make_async_remote_copy(
            slots.at[spot], slots.at[spot], sum_sem.at[0], sum_sem.at[1], device_id=chip(*at, 0), device_id_type=MESH
        )

    def plane_all(count):
        some = slots.at[pl.ds(0, count)]
        return pltpu.make_async_remote_copy(
            some, some, sum_sem.at[0], sum_sem.at[1], device_id=chip(0, 0, 1, 0), device_id_type=MESH
        )

    def column_copy(at, core):
        return pltpu.make_async_remote_copy(
            planes.at[z], planes.at[z], sum_sem.at[2], sum_sem.at[3], device_id=chip(*at, core), device_id_type=MESH
        )

    def column_all(ref, count):
        some = ref.at[pl.ds(0, count)]
        return pltpu.make_async_remote_copy(
            some, some, sum_sem.at[2], sum_sem.at[3], device_id=chip(0, 0, 1, 0), device_id_type=MESH
        )

    def add_up(ref, count):
        parts = [ref[i] for i in range(count)]
        while len(parts) > 1:
            parts = [a + b for a, b in zip(parts[::2], parts[1::2])]
        return parts[0]

    spot = 16 * c + x * 4 + q
    slots[spot] = packed
    far = sorted(plane, key=lambda at: -sum(min(d, 4 - d) for d in at))

    @pl.when(c == 1)
    def _():
        for at in far:
            plane_copy(at, spot).start()
        column_all(planes, 8).wait_recv()

    @pl.when(c == 0)
    def _():
        for at in far[:-1]:
            plane_copy(at, spot).start()
        plane_all(31).wait_recv()
        planes[z] = add_up(slots, 32)
        for dz in (4, 3, 5, 2, 6, 1, 7):
            column_copy((dz, 0, 0), 1).start()
            column_copy((dz, 0, 0), 0).start()
        column_copy((0, 0, 0), 1).start()
        column_all(planes, 7).wait_recv()

    packed = add_up(planes, 8)
    products_out[...] = packed

    @pl.when(c == 0)
    def _():
        plane_all(15).wait_send()
        column_all(slots, 15).wait_send()

    @pl.when(c == 1)
    def _():
        plane_all(16).wait_send()

    for d in range(4):
        for h in range(2):
            if d > 0:
                y_copy(d, h).wait_send()

            @pl.when(sends[h])
            def _():
                x_copy(d, h).wait_send()

    for side in range(2):

        @pl.when(sends[side])
        def _():
            for copy in side_copies(side):
                copy.wait_send()
    krylov_copy.wait()


def normalize(packed_ref, pairs, krylov, basis, block, proj, factor, w, bas, cf, in_sem, out_sem):
    def arrive(v):
        return (
            pltpu.make_async_copy(basis.at[:, v], bas.at[:, v], in_sem.at[0, v]),
            pltpu.make_async_copy(krylov.at[:, v], w.at[:, v], in_sem.at[1, v]),
        )

    def leave(v):
        return pltpu.make_async_copy(w.at[:, v], block.at[:, v], out_sem.at[v])

    for v in range(VARS):
        for copy in arrive(v):
            copy.start()

    sub = lax.broadcasted_iota(jnp.int32, (8, 128), 0)
    lane = lax.broadcasted_iota(jnp.int32, (8, 128), 1)
    packed = packed_ref[...] / TOTAL

    def lanes(index):
        return take(jnp.broadcast_to(packed[0:1], index.shape), index)

    proj[...] = lanes(jnp.where(lane < NB, NZ * (sub % 4) + lane, 0))[0:S, 0:NB]

    s_row = lax.broadcasted_iota(jnp.int32, (16, 128), 0) // 4
    t_row = lax.broadcasted_iota(jnp.int32, (16, 128), 0) % 4
    lane16 = lax.broadcasted_iota(jnp.int32, (16, 128), 1)
    place = jnp.where(lane16 < NB, lane16, 0)
    terms = jnp.where(lane16 < NB, -2.0 * lanes(place + NZ * s_row) * lanes(place + NZ * t_row), 0.0)
    for i in range(2):
        a = jnp.broadcast_to(pairs[i : i + 1, :], (16, 128))
        b = jnp.broadcast_to(pairs[2 + i : 3 + i, :], (16, 128))
        both = lanes(a + NZ * s_row) * lanes(b + NZ * t_row) + lanes(a + NZ * t_row) * lanes(b + NZ * s_row)
        terms = terms + packed[1 + i : 2 + i] * both
    whole = jnp.sum(terms, axis=1, keepdims=True)
    whole = whole + lanes(NZ * jnp.maximum(s_row, t_row) + NB + jnp.minimum(s_row, t_row))
    gram = [[jnp.broadcast_to(whole[4 * s + t : 4 * s + t + 1], (8, 128)) for t in range(S)] for s in range(S)]

    lower = [[None] * S for _ in range(S)]
    inverse = [[None] * S for _ in range(S)]
    for j in range(S):
        value = gram[j][j]
        for k in range(j):
            value = value - lower[j][k] * lower[j][k]
        lower[j][j] = jnp.sqrt(value)
        inverse[j][j] = 1.0 / lower[j][j]
        for i in range(j + 1, S):
            value = gram[i][j]
            for k in range(j):
                value = value - lower[i][k] * lower[j][k]
            lower[i][j] = value * inverse[j][j]
    for j in range(S):
        for i in range(j + 1, S):
            value = lower[i][j] * inverse[j][j]
            for k in range(j + 1, i):
                value = value + lower[i][k] * inverse[k][j]
            inverse[i][j] = -inverse[i][i] * value
    upper_factor = jnp.zeros((8, 128), F32)
    for s in range(S):
        for t in range(s + 1):
            upper_factor = jnp.where(jnp.logical_and(sub == t, lane == s), lower[s][t], upper_factor)
    factor[...] = upper_factor[0:S, 0:S]

    row24 = lax.broadcasted_iota(jnp.int32, (NZ, 128), 0)
    coefs = [lanes(row24 + NZ * k) for k in range(S)]

    for s in range(S):
        value = None
        for t in range(s + 1):
            term = coefs[t] * inverse[s][t][0:1]
            value = term if value is None else value + term
        cf[s] = -value
        for t in range(s + 1):
            cf[s, NB + t : NB + t + 1] = inverse[s][t][0:1]

    def finish(v, carry):
        for copy in arrive(v):
            copy.wait()

        def weight(s, n):
            return jnp.broadcast_to(cf[s, n : n + 1], (8, 128))

        totals = [[None] * LAYERS for _ in range(S)]
        for n in range(NZ):
            vectors = [(w[n - NB, v, l] if n >= NB else bas[n, v, l]) for l in range(LAYERS)]
            for s in range(S):
                if n >= NB and n - NB > s:
                    continue
                m = weight(s, n)
                for l in range(LAYERS):
                    term = m * vectors[l]
                    totals[s][l] = term if totals[s][l] is None else totals[s][l] + term
        for s in range(S):
            for l in range(LAYERS):
                w[s, v, l] = totals[s][l]
        leave(v).start()
        return carry

    lax.fori_loop(0, VARS, finish, 0)

    for v in range(VARS):
        leave(v).wait()


def shards(start, shifted_diag, face_coef, mixing, neighbours, basis):
    view = start.reshape(4, VARS, LAYERS, 2, 128).transpose(1, 2, 3, 0, 4).reshape(VARS, LAYERS, 8, 128)
    vectors = basis.reshape(NB, 4, VARS, LAYERS, 2, 128).transpose(0, 2, 3, 4, 1, 5)
    vectors = vectors.reshape(NB, VARS, LAYERS, 8, 128)
    hbm = pl.BlockSpec(memory_space=pltpu.HBM)
    vmem = pl.BlockSpec(memory_space=pltpu.VMEM)
    dma = pltpu.SemaphoreType.DMA
    krylov, packed = pl.pallas_call(
        kernel,
        out_shape=(
            jax.ShapeDtypeStruct((S, VARS, LAYERS, 8, 128), F32),
            jax.ShapeDtypeStruct((4, 128), F32),
        ),
        in_specs=[hbm] * 7,
        out_specs=(hbm, vmem),
        scratch_shapes=[
            pltpu.VMEM((4, 4, VARS, WIDE, 8, 128), F32),
            pltpu.VMEM((VARS, WIDE, 8, 128), F32),
            pltpu.VMEM((S, VARS, LAYERS, 8, 128), F32),
            pltpu.VMEM((NB, VARS, LAYERS, 8, 128), F32),
            pltpu.VMEM((FACES, LAYERS * FACE), F32),
            pltpu.VMEM((FACES, LAYERS * FACE), jnp.int32),
            pltpu.VMEM((16, 128), F32),
            pltpu.VMEM((2, FACES, 3 * FACE), F32),
            pltpu.VMEM((2, FACES, 3 * FACE), jnp.int32),
            pltpu.VMEM((2, 16, 128), F32),
            pltpu.VMEM((VARS, VARS), F32),
            pltpu.VMEM((4, 8 * S, 24 * S), F32),
            pltpu.VMEM((4, WIDE, 8, 128), F32),
            pltpu.VMEM((WIDE, 2, FACE, FACE), BF16),
            pltpu.VMEM((VARS * VARS, 8, 128), F32),
            pltpu.VMEM((22, 8, 128), F32),
            pltpu.VMEM((32, 4, 128), F32),
            pltpu.VMEM((8, 4, 128), F32),
            dma((7,)),
            dma((4, 2)),
            dma((4, 2)),
            dma((4, 2)),
            dma((4, 2)),
            dma((2, 3)),
            dma((2, 3)),
            dma((4,)),
            dma((1,)),
        ],
        compiler_params=pltpu.CompilerParams(
            collective_id=0, has_side_effects=True, vmem_limit_bytes=56 * 1024 * 1024
        ),
        name="krylov_block",
    )(view, face_coef, neighbours, shifted_diag.reshape(16, 128), vectors, mixing, jnp.asarray(time_tables()))
    block, proj, factor = pl.pallas_call(
        normalize,
        out_shape=(
            jax.ShapeDtypeStruct((S, VARS, LAYERS, 8, 128), F32),
            jax.ShapeDtypeStruct((S, NB), F32),
            jax.ShapeDtypeStruct((S, S), F32),
        ),
        in_specs=[vmem, vmem, hbm, hbm],
        out_specs=(hbm, vmem, vmem),
        scratch_shapes=[
            pltpu.VMEM((S, VARS, LAYERS, 8, 128), F32),
            pltpu.VMEM((NB, VARS, LAYERS, 8, 128), F32),
            pltpu.VMEM((S, NZ, 128), F32),
            dma((2, VARS)),
            dma((VARS,)),
        ],
        compiler_params=pltpu.CompilerParams(vmem_limit_bytes=56 * 1024 * 1024),
        name="normalize",
    )(packed, jnp.asarray(pair_table()), krylov, vectors)
    block = block.reshape(S, VARS, LAYERS, 2, 4, 128).transpose(0, 4, 1, 2, 3, 5)
    return block.reshape(S, 4, VARS, LAYERS * FACE), proj.T, factor


def solution(mesh):
    return jax.shard_map(
        shards,
        mesh=mesh,
        in_specs=(
            P("inst", None, "space"),
            P("space"),
            P(None, "space"),
            P(),
            P(None, "space"),
            P(None, "inst", None, "space"),
        ),
        out_specs=(P(None, "inst", None, "space"), P(), P()),
        check_vma=False,
    )
```

```python
import math

import jax
import jax.numpy as jnp
import numpy as np
from jax import lax
from jax.experimental import pallas as pl
from jax.experimental.pallas import tpu as pltpu
from jax.sharding import PartitionSpec as P

NT = 16
VARS = 7
NB = 20
S = 4
FACES = 6
FACE = 256
LAYERS = 8
NZ = NB + S
WIDE = 16
MESH = pl.DeviceIdType.MESH
F32 = jnp.float32
BF16 = jnp.bfloat16
TOTAL = float(NT * VARS * 131072)


GATHER = lax.GatherDimensionNumbers(
    offset_dims=(),
    collapsed_slice_dims=(1,),
    start_index_map=(1,),
    operand_batching_dims=(0,),
    start_indices_batching_dims=(0,),
)


def time_tables():
    n = np.arange(NT)
    diff = n[:, None] - n[None, :]
    angle = np.where(diff == 0, 1.0, np.pi * diff / NT)
    dmat = np.where(diff == 0, 0.0, 0.5 * (-1.0) ** diff * np.cos(angle) / np.sin(angle))
    tables = np.zeros((4, 8 * S, 8 * S))
    for d in range(4):
        for k in range(1, S + 1):
            for j in range(k):
                power = np.linalg.matrix_power(0.1 * dmat, k - j)
                part = math.comb(k, j) * power[:4, 4 * d : 4 * d + 4]
                for half in range(2):
                    r, c = (k - 1) * 8 + half * 4, j * 8 + half * 4
                    tables[d, r : r + 4, c : c + 4] = part
    high = tables.astype(jnp.bfloat16).astype(np.float64)
    low = (tables - high).astype(jnp.bfloat16).astype(np.float64)
    return np.concatenate([high, high, low], axis=2).astype(np.float32)


def basis_parts():
    blocks = {}
    for a in range(NB):
        for b in range(a, NB):
            blocks.setdefault((a // 8, b // 5), []).append((a, b))
    blocks[1, 1] += blocks.pop((2, 3))
    parts, at = [], 0
    for pairs in blocks.values():
        parts.append((pairs, at))
        at += -(-len(pairs) // 16)
    return parts


PARTS = basis_parts()


def spot_of(b):
    return b + 38 * (b >= 10)


def pair_table():
    table = np.zeros((2, 256), np.int32)
    for pairs, at in PARTS:
        for i, pair in enumerate(pairs):
            table[:, 16 * at + i] = [spot_of(b) for b in pair]
    return table.reshape(4, 128)


def take(x, index):
    return lax.gather(
        x, index[:, :, None], GATHER, slice_sizes=(1, 1), mode=lax.GatherScatterMode.PROMISE_IN_BOUNDS
    )


def kernel(
    start, coef, near, diag, basis, mixing, times,
    krylov, products_out,
    u, u4, w, bas, coef_own, near_own, diag_own, coef_side, near_side, diag_side,
    mixing_own, tables, geo, weights, mix, sums, slots, planes,
    load_sem, ys, yr, xs, xr, gs, gr, sum_sem, out_sem,
):
    p, q = lax.axis_index("space"), lax.axis_index("inst")
    z, x, c = p // 8, (p // 2) % 4, p % 2
    has_low, has_high = p > 0, p < 63
    y_up, y_down = (q + 1) % 4, (q + 3) % 4

    def chip(dz, dx, dy, core):
        return {"space": ((z + dz) % 8 * 4 + (x + dx) % 4) * 2 + core, "inst": (q + dy) % 4}

    plane = [(0, dx, dy) for dx in range(4) for dy in range(4)]
    column = [(dz, 0, 0) for dz in range(8)]

    loads = [
        pltpu.make_async_copy(coef, coef_own, load_sem.at[0]),
        pltpu.make_async_copy(near, near_own, load_sem.at[1]),
        pltpu.make_async_copy(diag, diag_own, load_sem.at[2]),
        pltpu.make_async_copy(mixing, mixing_own, load_sem.at[3]),
        pltpu.make_async_copy(start, u.at[0, 0, :, pl.ds(4, LAYERS)], load_sem.at[4]),
        pltpu.make_async_copy(times, tables, load_sem.at[5]),
        pltpu.make_async_copy(basis, bas, load_sem.at[6]),
    ]
    for copy in loads:
        copy.start()

    barrier = pltpu.get_barrier_semaphore()

    def greet(to):
        pl.semaphore_signal(barrier, inc=1, device_id=to, device_id_type=MESH)

    @pl.when(c == 0)
    def _():
        for at in column[1:]:
            greet(chip(*at, 0))
        for at in plane[1:]:
            greet(chip(*at, 0))
        for at in plane:
            greet(chip(*at, 1))

        @pl.when(jnp.logical_and(x == 0, z > 0))
        def _():
            greet({"space": p - 1, "inst": q})

    @pl.when(c == 1)
    def _():
        for at in column:
            greet(chip(*at, 0))
        greet({"space": p, "inst": y_up})
        greet({"space": p, "inst": y_down})

        @pl.when(has_high)
        def _():
            greet({"space": p + 1, "inst": q})

    def y_copy(d, h):
        dst = u.at[0, d, :, pl.ds(4 + 4 * h, 4)]
        if d == 2:
            src = u.at[0, 3 if h == 0 else 1, :, pl.ds(4 + 4 * h, 4)]
            to = y_up if h == 0 else y_down
        else:
            src = start.at[:, pl.ds(4 * h, 4)]
            to = y_up if d == 3 else y_down
        return pltpu.make_async_remote_copy(
            src, dst, ys.at[d, h], yr.at[d, h], device_id={"space": p, "inst": to}, device_id_type=MESH
        )

    def x_copy(d, side):
        count = 4 if d == 0 else 3
        if side == 0:
            dst = u.at[0, d, :, pl.ds(4 - count, count)]
            src = start.at[:, pl.ds(8 - count, count)] if d == 0 else u.at[0, d, :, pl.ds(12 - count, count)]
            to = p + 1
        else:
            dst = u.at[0, d, :, pl.ds(12, count)]
            src = start.at[:, pl.ds(0, count)] if d == 0 else u.at[0, d, :, pl.ds(4, count)]
            to = p - 1
        return pltpu.make_async_remote_copy(
            src, dst, xs.at[d, side], xr.at[d, side], device_id={"space": to, "inst": q}, device_id_type=MESH
        )

    def side_copies(side):
        to = p + 1 if side == 0 else p - 1
        cut = pl.ds(5 * FACE, 3 * FACE) if side == 0 else pl.ds(0, 3 * FACE)
        pairs = (
            (coef.at[:, cut], coef_side.at[side]),
            (near.at[:, cut], near_side.at[side]),
            (diag, diag_side.at[side]),
        )
        return [
            pltpu.make_async_remote_copy(
                src, dst, gs.at[side, i], gr.at[side, i], device_id={"space": to, "inst": q}, device_id_type=MESH
            )
            for i, (src, dst) in enumerate(pairs)
        ]

    sends = (has_high, has_low)
    hears = (has_low, has_high)

    def x_start(d, side):
        @pl.when(sends[side])
        def _():
            x_copy(d, side).start()

    sub = lax.broadcasted_iota(jnp.int32, (8, 128), 0)
    lane = lax.broadcasted_iota(jnp.int32, (8, 128), 1)
    upper = sub >= 4

    for copy in loads[:4]:
        copy.wait()

    matrix = mixing_own[...]
    for i in range(VARS):
        for j in range(VARS):
            mix[i * VARS + j] = jnp.broadcast_to(matrix[i : i + 1, j : j + 1], (8, 128))

    def spread(values, at):
        first = jnp.broadcast_to(values[:, at : at + 128], (8, 128))
        second = jnp.broadcast_to(values[:, at + 128 : at + 256], (8, 128))
        return jnp.where(upper, second, first)

    source = lax.broadcasted_iota(jnp.int32, (32, FACE), 0)

    def place(layer, coefs, nears, at, diags):
        values = [spread(coefs[f : f + 1], at) for f in range(FACES)]
        geo[0, layer] = sum(values[1:], values[0])
        geo[1, layer], geo[2, layer] = values[0], values[1]
        geo[3, layer] = jnp.where(
            upper, jnp.broadcast_to(diags[1:2], (8, 128)), jnp.broadcast_to(diags[0:1], (8, 128))
        )
        rows = [
            (nears[f : f + 1, at : at + FACE] & (FACE - 1), coefs[f : f + 1, at : at + FACE])
            for f in range(2, FACES)
        ]

        for r in range(0, FACE, 32):
            total = None
            for cells, values in rows:
                term = jnp.where(source + r == cells, values, 0.0)
                total = term if total is None else total + term
            high = total.astype(BF16)
            weights[layer, 0, pl.ds(r, 32)] = high
            weights[layer, 1, pl.ds(r, 32)] = (total - high.astype(F32)).astype(BF16)

    coefs, nears, diags = coef_own[...], near_own[...], diag_own[...]
    for layer in range(LAYERS):
        place(4 + layer, coefs, nears, layer * FACE, diags[2 * layer : 2 * layer + 2])
    def within(groups, layer):
        rows = []
        for values in groups:
            for i in range(0, VARS, 2):
                one = values[i]
                two = values[min(i + 1, VARS - 1)]
                first = jnp.where(upper, pltpu.roll(two, 4, 0), one)
                second = jnp.where(upper, two, pltpu.roll(one, 4, 0))
                rows.append(jnp.concatenate([first, second], axis=1))
        rows = jnp.concatenate(rows, axis=0)
        count = rows.shape[0]
        high = rows.astype(BF16)
        low = (rows - high.astype(F32)).astype(BF16)
        both = jnp.dot(jnp.concatenate([high, low], axis=0), weights[layer, 0], preferred_element_type=F32)
        out = both[0:count] + both[count:] + jnp.dot(high, weights[layer, 1], preferred_element_type=F32)
        results = []
        for at in range(0, count, 32):
            result = []
            for i in range(0, VARS, 2):
                first, second = (out[at + 4 * i : at + 4 * i + 8, e : e + 128] for e in (0, 128))
                if i + 1 == VARS:
                    result.append(jnp.where(upper, second, first))
                else:
                    result.append(jnp.where(upper, pltpu.roll(second, 4, 0), first))
                    result.append(jnp.where(upper, second, pltpu.roll(first, 4, 0)))
            results.append(result)
        return results

    def step(groups, j, layers):
        pairs = [(u.at[j, d], u4 if j == 3 else u.at[j + 1, d]) for d in groups]
        fluxes = []
        for b in layers:
            centers = [[src[v, b] for v in range(VARS)] for src, _ in pairs]
            inner = within(centers, b)
            g = [geo[f, b] for f in range(3)]
            for (src, _), center, inside in zip(pairs, centers, inner):
                fluxes.append(
                    [
                        g[0] * center[v] - g[1] * src[v, b - 1] - g[2] * src[v, b + 1] - inside[v]
                        for v in range(VARS)
                    ]
                )
        units = [(src, dst, b) for b in layers for src, dst in pairs]
        for i in range(VARS):
            totals = [geo[3, b] * src[i, b] for src, _, b in units]
            for n in range(VARS):
                m = mix[i * VARS + n]
                totals = [t + m * flux[n] for t, flux in zip(totals, fluxes)]
            for (_, dst, b), total in zip(units, totals):
                dst[i, b] = total

    def inside(*groups):
        for j in range(3):
            step(groups, j, range(5 + j, 11 - j))

    def outside(groups, j):
        reach = (4 if groups[0] == 0 else 3) - j
        step(groups, j, [*range(5 - reach, 5 + j), *range(11 - j, 11 + reach)])

    def combine(*groups):
        table = jnp.concatenate([tables[d] for d in groups], axis=1).astype(BF16)
        for v in range(VARS):
            stack = []
            for d in groups:
                parts = jnp.concatenate(
                    [jnp.concatenate([u[j, d, v, 4 + l] for l in range(LAYERS)], axis=1) for j in range(S)],
                    axis=0,
                )
                high = parts.astype(BF16)
                low = (parts - high.astype(F32)).astype(BF16)
                stack += [high, low, high]
            out = jnp.dot(table, jnp.concatenate(stack, axis=0), preferred_element_type=F32)
            for l in range(LAYERS):
                for k in range(S):
                    term = out[8 * k : 8 * k + 8, 128 * l : 128 * l + 128]
                    if groups[0] == 0:
                        last = u4[v, 4 + l] if k == S - 1 else u[k + 1, 0, v, 4 + l]
                        w[k, v, l] = last + term
                    else:
                        w[k, v, l] += term

    zero = jnp.zeros((8, 128), F32)

    def merge(parts, first=1, last=64):
        k = first
        while k <= last:
            bit = (lane // k) % 2 == 1
            merged = []
            for a, b in zip(parts[::2], parts[1::2]):
                if a is None and b is None:
                    merged.append(None)
                    continue
                a, b = zero if a is None else a, zero if b is None else b
                merged.append(jnp.where(bit, b, a) + pltpu.roll(jnp.where(bit, a, b), k, 1))
            parts, k = merged, 2 * k
        return parts[0]

    def sixteens(values, at):
        for i in range(0, len(values), 16):
            group = values[i : i + 16]
            sums[at + i // 16] = merge(group + [None] * (16 - len(group)), last=8)

    def row(at, count):
        total = merge([sums[at + i] for i in range(count)] + [None] * (8 - count), first=16)
        for k in (4, 2, 1):
            total = total + pltpu.roll(total, k, 0)
        return total

    def products(left, right, pairs):
        def body(v, totals):
            totals = list(totals)
            for l in range(LAYERS):
                a = {k: r[n, v, l] for k, (r, n) in left.items()}
                b = {k: r[n, v, l] for k, (r, n) in right.items()}
                totals = [t + a[m] * b[n] for t, (m, n) in zip(totals, pairs)]
            return tuple(totals)

        totals = lax.fori_loop(0, VARS, body, (zero,) * len(pairs))
        return dict(zip(pairs, totals))

    def basis_part(i):
        pairs, at = PARTS[i]
        totals = products(
            {a: (bas, a) for a, _ in pairs},
            {b: (bas, b) for _, b in pairs},
            pairs,
        )
        sixteens([(0.5 if a == b else 1.0) * totals[a, b] for a, b in pairs], at)

    def x_wait(d):
        for side in range(2):

            @pl.when(hears[side])
            def _():
                x_copy(d, side).wait_recv()

    loads[6].wait()
    for i in range(2):
        basis_part(i)

    @pl.when(c == 0)
    def _():
        pl.semaphore_wait(barrier, 30 + jnp.where(has_low, 1, 0))

    @pl.when(c == 1)
    def _():
        pl.semaphore_wait(barrier, 18 + jnp.where(jnp.logical_and(x == 3, z < 7), 1, 0))

    y_copy(3, 0).start()
    y_copy(1, 1).start()
    for side in range(2):

        @pl.when(sends[side])
        def _():
            for copy in side_copies(side):
                copy.start()

        x_start(0, side)
    y_copy(3, 1).start()
    y_copy(1, 0).start()

    for side in range(2):

        @pl.when(jnp.logical_not(hears[side]))
        def _():
            coef_side[side] = jnp.zeros((FACES, 3 * FACE), F32)
            near_side[side] = jnp.zeros((FACES, 3 * FACE), jnp.int32)
            diag_side[side] = jnp.zeros((16, 128), F32)
            for d in range(4):
                first = 0 if side == 0 else 12
                u[0, d, :, pl.ds(first, 4)] = jnp.zeros((VARS, 4, 8, 128), F32)

    for i in range(2, len(PARTS)):
        basis_part(i)
    known = (row(0, 8), row(8, 8))
    loads[4].wait()
    loads[5].wait()
    inside(0)

    for side in range(2):

        @pl.when(hears[side])
        def _():
            for copy in side_copies(side):
                copy.wait_recv()

        coefs, nears, diags = coef_side[side], near_side[side], diag_side[side]
        for layer in range(3):
            first = 10 + 2 * layer if side == 0 else 2 * layer
            place((1 if side == 0 else 12) + layer, coefs, nears, layer * FACE, diags[first : first + 2])

    y_copy(3, 0).wait_recv()
    y_copy(2, 0).start()
    y_copy(1, 1).wait_recv()
    y_copy(2, 1).start()
    x_start(3, 1)
    x_start(1, 0)

    x_wait(0)
    outside((0,), 0)
    outside((0,), 1)

    y_copy(3, 1).wait_recv()
    x_start(3, 0)
    y_copy(1, 0).wait_recv()
    x_start(1, 1)

    outside((0,), 2)
    step((0,), 3, range(4, 12))
    combine(0)

    y_copy(2, 0).wait_recv()
    x_start(2, 1)
    y_copy(2, 1).wait_recv()
    x_start(2, 0)

    inside(3, 1)
    inside(2)

    x_wait(3)
    x_wait(1)
    for j in range(3):
        outside((3, 1), j)
    combine(3, 1)
    x_wait(2)
    for j in range(3):
        outside((2,), j)
    combine(2)
    krylov_copy = pltpu.make_async_copy(w, krylov, out_sem.at[0])
    krylov_copy.start()

    new = {k: (w, k) for k in range(S)}
    for first in (0, 10):
        some = range(first, first + 10)
        pairs = [(b, k) for k in range(S) for b in some]
        totals = products({b: (bas, b) for b in some}, new, pairs)
        sixteens([totals[pair] for pair in pairs], 16 + 3 * (first // 10))
    pairs = [(t, k) for k in range(S) for t in range(k + 1)]
    totals = products(new, new, pairs)
    sixteens([totals.get((t, k)) for k in range(S) for t in range(S)], 22)
    packed = jnp.where(sub == 0, row(16, 7), jnp.where(sub == 1, known[0], known[1]))[0:4]

    def plane_copy(at, spot):
        return pltpu.make_async_remote_copy(
            slots.at[spot], slots.at[spot], sum_sem.at[0], sum_sem.at[1], device_id=chip(*at, 0), device_id_type=MESH
        )

    def plane_all(count):
        some = slots.at[pl.ds(0, count)]
        return pltpu.make_async_remote_copy(
            some, some, sum_sem.at[0], sum_sem.at[1], device_id=chip(0, 0, 1, 0), device_id_type=MESH
        )

    def column_copy(at, core):
        return pltpu.make_async_remote_copy(
            planes.at[z], planes.at[z], sum_sem.at[2], sum_sem.at[3], device_id=chip(*at, core), device_id_type=MESH
        )

    def column_all(ref, count):
        some = ref.at[pl.ds(0, count)]
        return pltpu.make_async_remote_copy(
            some, some, sum_sem.at[2], sum_sem.at[3], device_id=chip(0, 0, 1, 0), device_id_type=MESH
        )

    def add_up(ref, count):
        parts = [ref[i] for i in range(count)]
        while len(parts) > 1:
            parts = [a + b for a, b in zip(parts[::2], parts[1::2])]
        return parts[0]

    spot = 16 * c + x * 4 + q
    slots[spot] = packed
    far = sorted(plane, key=lambda at: -sum(min(d, 4 - d) for d in at))

    @pl.when(c == 1)
    def _():
        for at in far:
            plane_copy(at, spot).start()
        column_all(planes, 8).wait_recv()

    @pl.when(c == 0)
    def _():
        for at in far[:-1]:
            plane_copy(at, spot).start()
        plane_all(31).wait_recv()
        planes[z] = add_up(slots, 32)
        for dz in (4, 3, 5, 2, 6, 1, 7):
            column_copy((dz, 0, 0), 1).start()
            column_copy((dz, 0, 0), 0).start()
        column_copy((0, 0, 0), 1).start()
        column_all(planes, 7).wait_recv()

    packed = add_up(planes, 8)
    products_out[...] = packed

    @pl.when(c == 0)
    def _():
        plane_all(15).wait_send()
        column_all(slots, 15).wait_send()

    @pl.when(c == 1)
    def _():
        plane_all(16).wait_send()

    for d in range(4):
        for h in range(2):
            if d > 0:
                y_copy(d, h).wait_send()

            @pl.when(sends[h])
            def _():
                x_copy(d, h).wait_send()

    for side in range(2):

        @pl.when(sends[side])
        def _():
            for copy in side_copies(side):
                copy.wait_send()
    krylov_copy.wait()


def normalize(packed_ref, pairs, krylov, basis, block, proj, factor, w, bas, cf, in_sem, out_sem):
    def arrive(v):
        return (
            pltpu.make_async_copy(basis.at[:, v], bas.at[:, v], in_sem.at[0, v]),
            pltpu.make_async_copy(krylov.at[:, v], w.at[:, v], in_sem.at[1, v]),
        )

    def leave(v):
        return pltpu.make_async_copy(w.at[:, v], block.at[:, v], out_sem.at[v])

    for v in range(VARS):
        for copy in arrive(v):
            copy.start()

    sub = lax.broadcasted_iota(jnp.int32, (8, 128), 0)
    lane = lax.broadcasted_iota(jnp.int32, (8, 128), 1)
    packed = packed_ref[...] / TOTAL

    def lanes(index):
        return take(jnp.broadcast_to(packed[0:1], index.shape), index)

    def spots(b):
        return b + jnp.where(b >= 10, 38, 0)

    proj[...] = lanes(jnp.where(lane < NB, 10 * (sub % 4) + spots(lane), 0))[0:S, 0:NB]

    s_row = lax.broadcasted_iota(jnp.int32, (16, 128), 0) // 4
    t_row = lax.broadcasted_iota(jnp.int32, (16, 128), 0) % 4
    lane16 = lax.broadcasted_iota(jnp.int32, (16, 128), 1)
    place = jnp.where(lane16 < NB, spots(lane16), 0)
    terms = jnp.where(lane16 < NB, -2.0 * lanes(place + 10 * s_row) * lanes(place + 10 * t_row), 0.0)
    for i in range(2):
        a = jnp.broadcast_to(pairs[i : i + 1, :], (16, 128))
        b = jnp.broadcast_to(pairs[2 + i : 3 + i, :], (16, 128))
        both = lanes(a + 10 * s_row) * lanes(b + 10 * t_row) + lanes(a + 10 * t_row) * lanes(b + 10 * s_row)
        terms = terms + packed[1 + i : 2 + i] * both
    whole = jnp.sum(terms, axis=1, keepdims=True)
    whole = whole + lanes(96 + 4 * jnp.maximum(s_row, t_row) + jnp.minimum(s_row, t_row))
    gram = [[jnp.broadcast_to(whole[4 * s + t : 4 * s + t + 1], (8, 128)) for t in range(S)] for s in range(S)]

    lower = [[None] * S for _ in range(S)]
    inverse = [[None] * S for _ in range(S)]
    for j in range(S):
        value = gram[j][j]
        for k in range(j):
            value = value - lower[j][k] * lower[j][k]
        lower[j][j] = jnp.sqrt(value)
        inverse[j][j] = 1.0 / lower[j][j]
        for i in range(j + 1, S):
            value = gram[i][j]
            for k in range(j):
                value = value - lower[i][k] * lower[j][k]
            lower[i][j] = value * inverse[j][j]
    for j in range(S):
        for i in range(j + 1, S):
            value = lower[i][j] * inverse[j][j]
            for k in range(j + 1, i):
                value = value + lower[i][k] * inverse[k][j]
            inverse[i][j] = -inverse[i][i] * value
    upper_factor = jnp.zeros((8, 128), F32)
    for s in range(S):
        for t in range(s + 1):
            upper_factor = jnp.where(jnp.logical_and(sub == t, lane == s), lower[s][t], upper_factor)
    factor[...] = upper_factor[0:S, 0:S]

    row24 = lax.broadcasted_iota(jnp.int32, (NZ, 128), 0)
    coefs = [lanes(jnp.where(row24 < NB, spots(row24), 0) + 10 * k) for k in range(S)]

    for s in range(S):
        value = None
        for t in range(s + 1):
            term = coefs[t] * inverse[s][t][0:1]
            value = term if value is None else value + term
        cf[s] = -value
        for t in range(s + 1):
            cf[s, NB + t : NB + t + 1] = inverse[s][t][0:1]

    def finish(v, carry):
        for copy in arrive(v):
            copy.wait()

        def weight(s, n):
            return jnp.broadcast_to(cf[s, n : n + 1], (8, 128))

        totals = [[None] * LAYERS for _ in range(S)]
        for n in range(NZ):
            vectors = [(w[n - NB, v, l] if n >= NB else bas[n, v, l]) for l in range(LAYERS)]
            for s in range(S):
                if n >= NB and n - NB > s:
                    continue
                m = weight(s, n)
                for l in range(LAYERS):
                    term = m * vectors[l]
                    totals[s][l] = term if totals[s][l] is None else totals[s][l] + term
        for s in range(S):
            for l in range(LAYERS):
                w[s, v, l] = totals[s][l]
        leave(v).start()
        return carry

    lax.fori_loop(0, VARS, finish, 0)

    for v in range(VARS):
        leave(v).wait()


def shards(start, shifted_diag, face_coef, mixing, neighbours, basis):
    view = start.reshape(4, VARS, LAYERS, 2, 128).transpose(1, 2, 3, 0, 4).reshape(VARS, LAYERS, 8, 128)
    vectors = basis.reshape(NB, 4, VARS, LAYERS, 2, 128).transpose(0, 2, 3, 4, 1, 5)
    vectors = vectors.reshape(NB, VARS, LAYERS, 8, 128)
    hbm = pl.BlockSpec(memory_space=pltpu.HBM)
    vmem = pl.BlockSpec(memory_space=pltpu.VMEM)
    dma = pltpu.SemaphoreType.DMA
    krylov, packed = pl.pallas_call(
        kernel,
        out_shape=(
            jax.ShapeDtypeStruct((S, VARS, LAYERS, 8, 128), F32),
            jax.ShapeDtypeStruct((4, 128), F32),
        ),
        in_specs=[hbm] * 7,
        out_specs=(hbm, vmem),
        scratch_shapes=[
            pltpu.VMEM((4, 4, VARS, WIDE, 8, 128), F32),
            pltpu.VMEM((VARS, WIDE, 8, 128), F32),
            pltpu.VMEM((S, VARS, LAYERS, 8, 128), F32),
            pltpu.VMEM((NB, VARS, LAYERS, 8, 128), F32),
            pltpu.VMEM((FACES, LAYERS * FACE), F32),
            pltpu.VMEM((FACES, LAYERS * FACE), jnp.int32),
            pltpu.VMEM((16, 128), F32),
            pltpu.VMEM((2, FACES, 3 * FACE), F32),
            pltpu.VMEM((2, FACES, 3 * FACE), jnp.int32),
            pltpu.VMEM((2, 16, 128), F32),
            pltpu.VMEM((VARS, VARS), F32),
            pltpu.VMEM((4, 8 * S, 24 * S), F32),
            pltpu.VMEM((4, WIDE, 8, 128), F32),
            pltpu.VMEM((WIDE, 2, FACE, FACE), BF16),
            pltpu.VMEM((VARS * VARS, 8, 128), F32),
            pltpu.VMEM((23, 8, 128), F32),
            pltpu.VMEM((32, 4, 128), F32),
            pltpu.VMEM((8, 4, 128), F32),
            dma((7,)),
            dma((4, 2)),
            dma((4, 2)),
            dma((4, 2)),
            dma((4, 2)),
            dma((2, 3)),
            dma((2, 3)),
            dma((4,)),
            dma((1,)),
        ],
        compiler_params=pltpu.CompilerParams(
            collective_id=0, has_side_effects=True, vmem_limit_bytes=56 * 1024 * 1024
        ),
        name="krylov_block",
    )(view, face_coef, neighbours, shifted_diag.reshape(16, 128), vectors, mixing, jnp.asarray(time_tables()))
    block, proj, factor = pl.pallas_call(
        normalize,
        out_shape=(
            jax.ShapeDtypeStruct((S, VARS, LAYERS, 8, 128), F32),
            jax.ShapeDtypeStruct((S, NB), F32),
            jax.ShapeDtypeStruct((S, S), F32),
        ),
        in_specs=[vmem, vmem, hbm, hbm],
        out_specs=(hbm, vmem, vmem),
        scratch_shapes=[
            pltpu.VMEM((S, VARS, LAYERS, 8, 128), F32),
            pltpu.VMEM((NB, VARS, LAYERS, 8, 128), F32),
            pltpu.VMEM((S, NZ, 128), F32),
            dma((2, VARS)),
            dma((VARS,)),
        ],
        compiler_params=pltpu.CompilerParams(vmem_limit_bytes=56 * 1024 * 1024),
        name="normalize",
    )(packed, jnp.asarray(pair_table()), krylov, vectors)
    block = block.reshape(S, VARS, LAYERS, 2, 4, 128).transpose(0, 4, 1, 2, 3, 5)
    return block.reshape(S, 4, VARS, LAYERS * FACE), proj.T, factor


def solution(mesh):
    return jax.shard_map(
        shards,
        mesh=mesh,
        in_specs=(
            P("inst", None, "space"),
            P("space"),
            P(None, "space"),
            P(),
            P(None, "space"),
            P(None, "inst", None, "space"),
        ),
        out_specs=(P(None, "inst", None, "space"), P(), P()),
        check_vma=False,
    )
```
